32 devices in a mesh: groups: 2 (over y), ctx: 8 (over z, x), chan: 2 (over core).
Axes of the slice: x: 2, y: 2, z: 4, core: 2. Of those that a mesh axis runs over, the one named last changes fastest.
Arguments:
- first_gate: bfloat16 [128, 8192], P('chan', ('groups', 'ctx')), parts along dimension 1, may hold values from -6 to 6
- second_gate: bfloat16 [128, 8192], P('chan', ('groups', 'ctx')), parts along dimension 1, may hold values from -6 to 6
- values: bfloat16 [128, 8192], P('chan', ('groups', 'ctx')), parts along dimension 1, may hold values from -6 to 6
- filters: float32 [128, 8192], P('chan', ('groups', 'ctx')), parts along dimension 1, may hold values from -0.09375 to 0.09375
- skip_gain: float32 [128], P('chan'), may hold values from -4 to 4
- grad_output: bfloat16 [128, 8192], P('chan', ('groups', 'ctx')), parts along dimension 1, may hold values from -6 to 6
Outputs:
- output: float32 [128, 8192], P('chan', ('groups', 'ctx')), parts along dimension 1
- grad_first: float32 [128, 8192], P('chan', ('groups', 'ctx')), parts along dimension 1
- grad_second: float32 [128, 8192], P('chan', ('groups', 'ctx')), parts along dimension 1
- grad_values: float32 [128, 8192], P('chan', ('groups', 'ctx')), parts along dimension 1
- grad_filters: float32 [128, 8192], P('chan', ('groups', 'ctx')), parts along dimension 1
- grad_skip: float32 [256], P(('groups', 'chan')), parts along dimension 0
The draws below stay inside these ranges and needn't reach their ends.
There are 2 independent parts, one for each index of `groups`. The reference program is written for one: setup_inputs(seed, part) draws one part's arguments, and reference() takes and returns one part's arrays. A program takes and returns all parts, laid end to end along the dimension named above; an argument that names none is the same for every part. Nothing has to cross between parts.
All inputs are finite; a program needn't handle non-finite values.
Results may differ from the reference program's by a relative error of at most 0.0003.
Values sent between devices are 32-bit elements; how exact they have to be, the bound alone decides.
No kernel may reach another device: no remote copies, remote signals or barrier semaphores. Data moves between devices by JAX's collectives and lax.ppermute only.
A program may use at most 64 MiB of HBM per device.

```python
import jax
import jax.numpy as jnp

CHANNELS = 128
TOK_DEV = 512
LENGTH = 4096
N_CTX = 8


def shard_levels(own_key, dims, split, smallest, high):
    level = 1.0
    for position, parts in split:
        steps = jax.random.uniform(jax.random.fold_in(jax.random.fold_in(own_key, 6), position), (parts,), jnp.float32, smallest / len(split), high / len(split))
        level = level * jnp.repeat(jnp.exp(steps), dims[position] // parts).reshape((-1,) + (1,) * (len(dims) - 1 - position))
    return level


def normal_values(own_key, extent, deviation, bound, cuts=(), dtype=jnp.bfloat16):
    values = jax.random.normal(own_key, extent, jnp.float32) * deviation
    if len(cuts) > 0:
        values = shard_levels(own_key, extent, cuts, -0.22, 0.18) * values
    return jnp.clip(values, min=-bound, max=bound).astype(dtype)


def setup_inputs(seed: int = 0, part: int = 0) -> dict:
    arg_keys = jax.random.split(jax.random.key(seed), 7)
    part_splits = jax.random.split(jax.random.fold_in(arg_keys[6], part), 7)
    first_gate = normal_values(part_splits[0], (CHANNELS, LENGTH), 1.0, 6.0, ((0, 2), (1, 8)))
    second_gate = normal_values(part_splits[1], (CHANNELS, LENGTH), 1.0, 6.0, ((0, 2), (1, 8)))
    values = normal_values(part_splits[2], (CHANNELS, LENGTH), 1.0, 6.0, ((0, 2), (1, 8)))
    filters = normal_values(part_splits[3], (CHANNELS, LENGTH), (TOK_DEV * N_CTX) ** -0.5, 0.09375, ((0, 2), (1, 8)), jnp.float32)
    skip_gain = normal_values(arg_keys[4], (CHANNELS,), 1.0, 4.0, ((0, 2),), jnp.float32)
    grad_output = normal_values(part_splits[5], (CHANNELS, LENGTH), 1.0, 6.0, ((0, 2), (1, 8)))
    return {"first_gate": first_gate, "second_gate": second_gate, "values": values, "filters": filters, "skip_gain": skip_gain, "grad_output": grad_output}


def reference(first_gate, second_gate, values, filters, skip_gain, grad_output):
    length = filters.shape[1]
    size = 2 * length
    first = first_gate.astype(jnp.float32)
    second = second_gate.astype(jnp.float32)
    values_wide = values.astype(jnp.float32)
    mixed = first * values_wide
    carried = grad_output.astype(jnp.float32) * second
    mixed_spec = jnp.fft.rfft(mixed, n=size, axis=1)
    filter_spec = jnp.fft.rfft(filters, n=size, axis=1)
    carry_spec = jnp.fft.rfft(carried, n=size, axis=1)
    convolved = jnp.fft.irfft(filter_spec * mixed_spec, n=size, axis=1)[:, :length]
    back_conv = jnp.fft.irfft(jnp.conj(filter_spec) * carry_spec, n=size, axis=1)[:, :length]
    grad_filters = jnp.fft.irfft(jnp.conj(mixed_spec) * carry_spec, n=size, axis=1)[:, :length]
    gain = skip_gain[:, None]
    before = convolved + gain * mixed
    output = second * before
    grad_second = grad_output.astype(jnp.float32) * before
    back_mixed = back_conv + gain * carried
    grad_first = back_mixed * values_wide
    grad_values = back_mixed * first
    grad_skip = jnp.sum(carried * mixed, axis=1)
    return (output.astype(jnp.float32), grad_first.astype(jnp.float32), grad_second.astype(jnp.float32),
            grad_values.astype(jnp.float32), grad_filters.astype(jnp.float32), grad_skip.astype(jnp.float32))
```

```python
import math

import jax
import jax.numpy as jnp
import numpy as np
from jax import lax
from jax.experimental import pallas as pl
from jax.experimental.pallas import tpu as pltpu
from jax.sharding import PartitionSpec as P

HIGHEST = lax.Precision.HIGHEST
LANES = 128
ROWS = 8
VMEM = pl.BlockSpec(memory_space=pltpu.VMEM)
PARAMS = pltpu.CompilerParams(vmem_limit_bytes=48 * 1024 * 1024)


def halves(table):
    high = table.astype(np.float32).astype(jnp.bfloat16)
    low = (table - high.astype(np.float64)).astype(np.float32).astype(jnp.bfloat16)
    return high, low


def make_tables(length):
    groups = length // LANES
    period = 2 * length
    turns = 2 * groups
    k1 = np.arange(groups + 1)
    inner = np.arange(1, groups)
    a = np.arange(groups)
    eye = np.eye(ROWS)
    angle = 2.0 * np.pi / turns
    outer = np.concatenate([np.cos(angle * (k1[:, None] * a % turns)), np.sin(angle * (inner[:, None] * a % turns))])
    weight = np.where((k1 == 0) | (k1 == groups), 1.0, 2.0) / period
    back = np.concatenate(
        [weight[:, None] * np.cos(angle * (k1[:, None] * a % turns)), -2.0 / period * np.sin(angle * (inner[:, None] * a % turns))]
    )
    b = np.arange(LANES)
    wave = 2.0 * np.pi / LANES * (b[:, None] * b % LANES)
    cosine, sine = np.cos(wave), np.sin(wave)
    lane_fwd = np.block([[cosine, -sine], [sine, cosine]])
    lane_back = np.block([[cosine, sine], [-sine, cosine]])
    twist = 2.0 * np.pi / period * (k1[:, None] * b % period)
    twist = np.repeat(twist, ROWS, axis=0)
    return (
        *halves(np.kron(outer, eye)),
        *halves(np.kron(back.T, eye)),
        *halves(lane_fwd),
        *halves(lane_back),
        np.cos(twist).astype(np.float32),
        np.sin(twist).astype(np.float32),
    )


def split(data):
    high = data.astype(jnp.bfloat16)
    return high, (data - high.astype(jnp.float32)).astype(jnp.bfloat16)


def dot(left, right):
    return jnp.dot(left, right, preferred_element_type=jnp.float32)


def table_left(high, low, data):
    data_high, data_low = split(data)
    return dot(high, data_high) + (dot(high, data_low) + dot(low, data_high))


def table_right(data, high, low):
    data_high, data_low = split(data)
    return dot(data_high, high) + (dot(data_low, high) + dot(data_high, low))


def gate_kernel(first_ref, second_ref, values_ref, filters_ref, grad_ref, out_ref):
    mixed = first_ref[...].astype(jnp.float32) * values_ref[...].astype(jnp.float32)
    carried = grad_ref[...].astype(jnp.float32) * second_ref[...].astype(jnp.float32)
    shards = out_ref.shape[0]
    tiles = filters_ref.shape[1] // LANES
    for s, signal in enumerate((mixed, filters_ref[...], carried)):
        for j in range(tiles):
            tile = signal[:, j * LANES : (j + 1) * LANES].reshape(shards, ROWS, LANES)
            row = (s * tiles + j) * ROWS
            out_ref[:, row : row + ROWS, :] = tile


def spectral_kernel(in_ref, oh, ol, bh, bl, fh, fl, ih, il, cos_ref, sin_ref, out_ref):
    shards = in_ref.shape[0]
    span = in_ref.shape[1] // 3
    rows = shards * span
    spec_rows = rows + ROWS
    signals = [in_ref[:, s * span : (s + 1) * span, :].reshape(rows, LANES) for s in range(3)]
    total = jnp.sum((signals[0] * signals[2]).reshape(rows // ROWS, ROWS, LANES), axis=0)
    total = jnp.broadcast_to(jnp.sum(total, axis=1, keepdims=True), (ROWS, LANES))
    out_ref[:, 3 * span :, :] = jnp.broadcast_to(total[None], (shards, ROWS, LANES))
    columns = table_left(oh[...], ol[...], jnp.concatenate(signals, axis=1))
    cosine, sine = cos_ref[...], sin_ref[...]
    edge = jnp.zeros((ROWS, LANES), jnp.float32)
    spectra = []
    for s in range(3):
        lanes = slice(s * LANES, (s + 1) * LANES)
        real = columns[:spec_rows, lanes]
        imag = jnp.concatenate([edge, columns[spec_rows:, lanes], edge], axis=0)
        turned = jnp.concatenate([real * cosine - imag * sine, -(real * sine + imag * cosine)], axis=1)
        spectra.append(table_right(turned, fh[...], fl[...]))
    (mr, mi), (fr, fi), (cr, ci) = [(x[:, :LANES], x[:, LANES:]) for x in spectra]
    products = (
        (fr * mr - fi * mi, fr * mi + fi * mr),
        (fr * cr + fi * ci, fr * ci - fi * cr),
        (mr * cr + mi * ci, mr * ci - mi * cr),
    )
    reverted = []
    for real, imag in products:
        waves = table_right(jnp.concatenate([real, imag], axis=1), ih[...], il[...])
        real, imag = waves[:, :LANES], waves[:, LANES:]
        turned_imag = real * sine + imag * cosine
        reverted.append(jnp.concatenate([real * cosine - imag * sine, turned_imag[ROWS:-ROWS]], axis=0))
    result = table_left(bh[...], bl[...], jnp.concatenate(reverted, axis=1))
    for s in range(3):
        out_ref[:, s * span : (s + 1) * span, :] = result[:, s * LANES : (s + 1) * LANES].reshape(shards, span, LANES)


def output_kernel(in_ref, first_ref, second_ref, values_ref, grad_ref, gain_ref, out_ref, gfirst_ref, gsecond_ref, gvalues_ref, gfilters_ref, gskip_ref):
    channels, blocks = first_ref.shape
    tiles = blocks // LANES
    first = first_ref[...].astype(jnp.float32)
    second = second_ref[...].astype(jnp.float32)
    values = values_ref[...].astype(jnp.float32)
    grad = grad_ref[...].astype(jnp.float32)
    diagonal = lax.broadcasted_iota(jnp.int32, (channels, channels), 0) == lax.broadcasted_iota(jnp.int32, (channels, channels), 1)
    gain = jnp.sum(jnp.where(diagonal, gain_ref[...], 0.0), axis=1, keepdims=True)
    result = []
    for s in range(3):
        parts = [in_ref[:, (s * tiles + j) * ROWS : (s * tiles + j + 1) * ROWS, :].reshape(channels, LANES) for j in range(tiles)]
        result.append(jnp.concatenate(parts, axis=1))
    before = result[0] + gain * (first * values)
    out_ref[...] = second * before
    gsecond_ref[...] = grad * before
    back = result[1] + gain * (grad * second)
    gfirst_ref[...] = back * values
    gvalues_ref[...] = back * first
    gfilters_ref[...] = result[2]
    total = in_ref[:, 3 * tiles * ROWS :, :].reshape(channels, LANES)[:, :channels]
    gskip_ref[...] = jnp.sum(jnp.where(diagonal, total, 0.0), axis=0, keepdims=True)


def by_channels(first_gate, second_gate, values, filters, skip_gain, grad_output):
    channels, blocks = filters.shape
    shards = lax.axis_size("ctx")
    tiles = blocks // LANES
    length = blocks * shards
    full = jax.ShapeDtypeStruct((channels, blocks), jnp.float32)
    slabs = pl.pallas_call(
        gate_kernel,
        out_shape=jax.ShapeDtypeStruct((shards, 3 * tiles * ROWS, LANES), jnp.float32),
        in_specs=[VMEM] * 5,
        out_specs=VMEM,
        compiler_params=PARAMS,
    )(first_gate, second_gate, values, filters, grad_output)
    slabs = lax.all_to_all(slabs, "ctx", split_axis=0, concat_axis=0, tiled=True)
    tables = make_tables(length)
    slabs = pl.pallas_call(
        spectral_kernel,
        out_shape=jax.ShapeDtypeStruct((shards, (3 * tiles + 1) * ROWS, LANES), jnp.float32),
        in_specs=[VMEM] * (1 + len(tables)),
        out_specs=VMEM,
        compiler_params=PARAMS,
    )(slabs, *tables)
    slabs = lax.all_to_all(slabs, "ctx", split_axis=0, concat_axis=0, tiled=True)
    *wide, grad_skip = pl.pallas_call(
        output_kernel,
        out_shape=(full,) * 5 + (jax.ShapeDtypeStruct((1, channels), jnp.float32),),
        in_specs=[VMEM] * 6,
        out_specs=(VMEM,) * 6,
        compiler_params=PARAMS,
    )(slabs, first_gate, second_gate, values, grad_output, skip_gain.reshape(1, channels))
    return (*wide, grad_skip.reshape(channels))


def turn_table(first_index, second_index, period):
    product = first_index[:, None] * second_index[None, :] % period
    angles = 2.0 * math.pi / period * product.astype(jnp.float32)
    return (jnp.cos(angles), jnp.sin(angles))


def right_dot(data, table):
    return jnp.dot(data, table, precision=HIGHEST)


def by_columns(first_gate, second_gate, values, filters, skip_gain, grad_output):
    channels, length = filters.shape
    shards = lax.axis_size("ctx")
    blocks = length // shards
    position = lax.axis_index("ctx")
    period = 2 * shards * length
    first = first_gate.astype(jnp.float32)
    second = second_gate.astype(jnp.float32)
    values_wide = values.astype(jnp.float32)
    mixed = first * values_wide
    carried = grad_output.astype(jnp.float32) * second
    signal = jnp.stack([mixed, filters, carried]).reshape(3, channels, blocks, shards)
    spread = lax.all_to_all(signal, "ctx", split_axis=3, concat_axis=3, tiled=True)
    shard_index = jnp.arange(shards, dtype=jnp.int32)
    cosine, sines = turn_table(shard_index, shard_index, 2 * shards)
    parity = (1 - 2 * (shard_index % 2)).astype(jnp.float32)
    fwd_real = jnp.stack([cosine, parity[:, None] * cosine], axis=1)
    fwd_imag = jnp.stack([-sines, -parity[:, None] * sines], axis=1)
    real_part = jnp.einsum("scbm,mjk->scjbk", spread, fwd_real, precision=HIGHEST)
    imag_part = jnp.einsum("scbm,mjk->scjbk", spread, fwd_imag, precision=HIGHEST)
    sectioned = jnp.stack([real_part, imag_part])
    moved = lax.all_to_all(sectioned, "ctx", split_axis=5, concat_axis=5, tiled=True).reshape(
        2, 3, channels, 2, length
    )
    col_real = moved[0]
    col_imag = moved[1]
    col_index = jnp.stack([position, position + shards])
    line_index = jnp.arange(length, dtype=jnp.int32)
    twist_cos, twist_sin = turn_table(col_index, line_index, period)
    turned_real = col_real * twist_cos + col_imag * twist_sin
    turned_imag = col_imag * twist_cos - col_real * twist_sin
    wave_cos, wave_sin = turn_table(line_index, line_index, length)
    spec_real = right_dot(turned_real, wave_cos) + right_dot(turned_imag, wave_sin)
    spec_imag = right_dot(turned_imag, wave_cos) - right_dot(turned_real, wave_sin)
    mixed_real, filter_real, carry_real = (spec_real[0], spec_real[1], spec_real[2])
    mixed_imag, filter_imag, carry_imag = (spec_imag[0], spec_imag[1], spec_imag[2])
    prod_real = jnp.stack(
        [
            filter_real * mixed_real - filter_imag * mixed_imag,
            filter_real * carry_real + filter_imag * carry_imag,
            mixed_real * carry_real + mixed_imag * carry_imag,
        ]
    )
    prod_imag = jnp.stack(
        [
            filter_real * mixed_imag + filter_imag * mixed_real,
            filter_real * carry_imag - filter_imag * carry_real,
            mixed_real * carry_imag - mixed_imag * carry_real,
        ]
    )
    back_real = right_dot(prod_real, wave_cos) - right_dot(prod_imag, wave_sin)
    back_imag = right_dot(prod_real, wave_sin) + right_dot(prod_imag, wave_cos)
    reverted_real = back_real * twist_cos - back_imag * twist_sin
    reverted_imag = back_real * twist_sin + back_imag * twist_cos
    packed = jnp.stack([reverted_real, reverted_imag])
    returned = lax.all_to_all(
        packed.reshape(2, 3, channels, 2, blocks, shards),
        "ctx",
        split_axis=5,
        concat_axis=5,
        tiled=True,
    )
    inv_real = jnp.stack([cosine, cosine * parity[None, :]])
    inv_imag = jnp.stack([-sines, -sines * parity[None, :]])
    timed = jnp.einsum("scjbk,jkm->scbm", returned[0], inv_real, precision=HIGHEST)
    timed = timed + jnp.einsum("scjbk,jkm->scbm", returned[1], inv_imag, precision=HIGHEST)
    timed = timed * (1.0 / period)
    result = lax.all_to_all(timed, "ctx", split_axis=3, concat_axis=3, tiled=True).reshape(
        3, channels, length
    )
    gain = skip_gain[:, None]
    before = result[0] + gain * mixed
    output = second * before
    grad_second = grad_output.astype(jnp.float32) * before
    back_mixed = result[1] + gain * carried
    grad_first = back_mixed * values_wide
    grad_values = back_mixed * first
    grad_filters = result[2]
    grad_skip = lax.psum(jnp.sum(carried * mixed, axis=1), "ctx")
    return (output, grad_first, grad_second, grad_values, grad_filters, grad_skip)


def per_device(first_gate, second_gate, values, filters, skip_gain, grad_output):
    channels, blocks = filters.shape
    shards = lax.axis_size("ctx")
    fits = channels == ROWS * shards and blocks % LANES == 0 and channels <= LANES
    plan = by_channels if fits else by_columns
    return plan(first_gate, second_gate, values, filters, skip_gain, grad_output)


def solution(mesh):
    placed = (
        P("chan", ("groups", "ctx")),
        P("chan", ("groups", "ctx")),
        P("chan", ("groups", "ctx")),
        P("chan", ("groups", "ctx")),
        P("chan"),
        P("chan", ("groups", "ctx")),
    )
    return jax.shard_map(
        per_device,
        mesh=mesh,
        in_specs=placed,
        out_specs=(
            P("chan", ("groups", "ctx")),
            P("chan", ("groups", "ctx")),
            P("chan", ("groups", "ctx")),
            P("chan", ("groups", "ctx")),
            P("chan", ("groups", "ctx")),
            P(("groups", "chan")),
        ),
        check_vma=False,
    )
```

```python
import math

import jax
import jax.numpy as jnp
import numpy as np
from jax import lax
from jax.experimental import pallas as pl
from jax.experimental.pallas import tpu as pltpu
from jax.sharding import PartitionSpec as P

HIGHEST = lax.Precision.HIGHEST
LANES = 128
ROWS = 8
VMEM = pl.BlockSpec(memory_space=pltpu.VMEM)
PARAMS = pltpu.CompilerParams(vmem_limit_bytes=48 * 1024 * 1024)


def make_tables(length):
    groups = length // LANES
    period = 2 * length
    turns = 2 * groups
    k1 = np.arange(groups + 1)
    inner = k1[1:-1]
    a = np.arange(groups)
    b = np.arange(LANES)
    cosine = np.cos(2.0 * np.pi / turns * (k1[:, None] * a % turns))
    sine = np.sin(2.0 * np.pi / turns * (inner[:, None] * a % turns))
    weight = np.where((k1 == 0) | (k1 == groups), 1.0, 2.0) / period
    outer = np.concatenate([cosine, sine])
    back = np.concatenate([weight[:, None] * cosine, -2.0 / period * sine]).T
    wave = 2.0 * np.pi / LANES * (b[:, None] * b % LANES)
    twist = 2.0 * np.pi / period * (k1[:, None] * b % period)
    parts = [np.repeat(outer, ROWS, axis=1), np.repeat(back, ROWS, axis=1)]
    parts = [np.concatenate(np.split(part, part.shape[1] // LANES, axis=1)) for part in parts]
    parts += [np.cos(wave), np.sin(wave), np.cos(twist), np.sin(twist)]
    parts.append(np.zeros((-2 * (groups + 1) % ROWS, LANES)))
    return np.concatenate(parts).astype(np.float32)


def spread_rows(table, masked):
    rows, columns = table.shape
    wide = jnp.broadcast_to(table[:, None, :], (rows, ROWS, columns))
    if masked:
        shape = (ROWS, columns)
        own = lax.broadcasted_iota(jnp.int32, shape, 0) == lax.broadcasted_iota(jnp.int32, shape, 1) % ROWS
        wide = jnp.where(own[None], wide, 0.0)
    return wide.reshape(rows * ROWS, columns)


def split(data):
    high = data.astype(jnp.bfloat16)
    return high, (data - high.astype(jnp.float32)).astype(jnp.bfloat16)


def dot(left, right):
    return jnp.dot(left, right, preferred_element_type=jnp.float32)


def long_dot(left, right):
    return dot(left[0], right[0]) + (dot(left[0], right[1]) + dot(left[1], right[0]))


def read_tables(table_ref, groups):
    tiles = groups * ROWS // LANES
    row = 0

    def take(rows, pieces=1):
        nonlocal row
        parts = [table_ref[row + i * rows : row + (i + 1) * rows, :] for i in range(pieces)]
        row += rows * pieces
        return jnp.concatenate(parts, axis=1)

    outer = split(spread_rows(take(2 * groups, tiles), True))
    back = split(spread_rows(take(groups, 2 * tiles), True))
    cosine, sine = split(take(LANES)), split(take(LANES))
    forward, inverse = [], []
    for c, s in zip(cosine, sine):
        forward.append(jnp.concatenate([jnp.concatenate([c, -s], axis=1), jnp.concatenate([s, c], axis=1)], axis=0))
        inverse.append(jnp.concatenate([jnp.concatenate([c, s], axis=1), jnp.concatenate([-s, c], axis=1)], axis=0))
    twist = (spread_rows(take(groups + 1), False), spread_rows(take(groups + 1), False))
    return outer, back, forward, inverse, twist


def spectral_kernel(in_ref, table_ref, out_ref):
    shards = in_ref.shape[0]
    tiles = in_ref.shape[3] // LANES
    span = tiles * ROWS
    rows = shards * span
    spec_rows = rows + ROWS
    outer, back, forward, inverse, (cosine, sine) = read_tables(table_ref, rows // ROWS)

    def take(s):
        parts = [in_ref[:, s, :, j * LANES : (j + 1) * LANES] for j in range(tiles)]
        return jnp.stack(parts, axis=1).reshape(rows, LANES)

    signals = [take(s) for s in range(3)]
    total = jnp.sum((signals[0] * signals[2]).reshape(rows // ROWS, ROWS, LANES), axis=0)
    total = jnp.broadcast_to(jnp.sum(total, axis=1, keepdims=True), (ROWS, LANES))
    out_ref[:, 3 * span :, :] = jnp.broadcast_to(total[None], (shards, ROWS, LANES))
    columns = long_dot(outer, split(jnp.concatenate(signals, axis=1)))
    edge = jnp.zeros((ROWS, LANES), jnp.float32)
    spectra = []
    for s in range(3):
        lanes = slice(s * LANES, (s + 1) * LANES)
        real = columns[:spec_rows, lanes]
        imag = jnp.concatenate([edge, columns[spec_rows:, lanes], edge], axis=0)
        turned = jnp.concatenate([real * cosine - imag * sine, -(real * sine + imag * cosine)], axis=1)
        spectra.append(long_dot(split(turned), forward))
    (mr, mi), (fr, fi), (cr, ci) = [(x[:, :LANES], x[:, LANES:]) for x in spectra]
    products = (
        (fr * mr - fi * mi, fr * mi + fi * mr),
        (fr * cr + fi * ci, fr * ci - fi * cr),
        (mr * cr + mi * ci, mr * ci - mi * cr),
    )
    reverted = []
    for real, imag in products:
        waves = long_dot(split(jnp.concatenate([real, imag], axis=1)), inverse)
        real, imag = waves[:, :LANES], waves[:, LANES:]
        turned_imag = real * sine + imag * cosine
        reverted.append(jnp.concatenate([real * cosine - imag * sine, turned_imag[ROWS:-ROWS]], axis=0))
    result = long_dot(back, split(jnp.concatenate(reverted, axis=1)))
    for s in range(3):
        out_ref[:, s * span : (s + 1) * span, :] = result[:, s * LANES : (s + 1) * LANES].reshape(shards, span, LANES)


def output_kernel(in_ref, first_ref, second_ref, values_ref, grad_ref, out_ref, gfirst_ref, gsecond_ref, gvalues_ref, gfilters_ref, gskip_ref):
    channels, blocks = out_ref.shape
    tiles = blocks // LANES

    def take(s):
        parts = [in_ref[:, (s * tiles + j) * ROWS : (s * tiles + j + 1) * ROWS, :].reshape(channels, LANES) for j in range(tiles)]
        return jnp.concatenate(parts, axis=1)

    before = take(0)
    out_ref[...] = second_ref[...].astype(jnp.float32) * before
    gsecond_ref[...] = grad_ref[...].astype(jnp.float32) * before
    back = take(1)
    gfirst_ref[...] = back * values_ref[...].astype(jnp.float32)
    gvalues_ref[...] = back * first_ref[...].astype(jnp.float32)
    gfilters_ref[...] = take(2)
    diagonal = lax.broadcasted_iota(jnp.int32, (channels, channels), 0) == lax.broadcasted_iota(jnp.int32, (channels, channels), 1)
    total = in_ref[:, 3 * tiles * ROWS :, :].reshape(channels, LANES)[:, :channels]
    gskip_ref[...] = jnp.sum(jnp.where(diagonal, total, 0.0), axis=0, keepdims=True)


def by_channels(first_gate, second_gate, values, filters, skip_gain, grad_output):
    channels, blocks = filters.shape
    shards = lax.axis_size("ctx")
    tiles = blocks // LANES
    length = blocks * shards
    full = jax.ShapeDtypeStruct((channels, blocks), jnp.float32)
    mixed = first_gate.astype(jnp.float32) * values.astype(jnp.float32)
    carried = grad_output.astype(jnp.float32) * second_gate.astype(jnp.float32)
    first_tap = (lax.broadcasted_iota(jnp.int32, filters.shape, 1) == 0) & (lax.axis_index("ctx") == 0)
    filters = filters + jnp.where(first_tap, skip_gain[:, None], 0.0)
    slabs = jnp.stack([x.reshape(shards, ROWS, blocks) for x in (mixed, filters, carried)], axis=1)
    slabs = lax.all_to_all(slabs, "ctx", split_axis=0, concat_axis=0, tiled=True)
    slabs = pl.pallas_call(
        spectral_kernel,
        out_shape=jax.ShapeDtypeStruct((shards, (3 * tiles + 1) * ROWS, LANES), jnp.float32),
        in_specs=[VMEM] * 2,
        out_specs=VMEM,
        compiler_params=PARAMS,
    )(slabs, make_tables(length))
    slabs = lax.all_to_all(slabs, "ctx", split_axis=0, concat_axis=0, tiled=True)
    *wide, grad_skip = pl.pallas_call(
        output_kernel,
        out_shape=(full,) * 5 + (jax.ShapeDtypeStruct((1, channels), jnp.float32),),
        in_specs=[VMEM] * 5,
        out_specs=(VMEM,) * 6,
        compiler_params=PARAMS,
    )(slabs, first_gate, second_gate, values, grad_output)
    return (*wide, grad_skip.reshape(channels))


def turn_table(first_index, second_index, period):
    product = first_index[:, None] * second_index[None, :] % period
    angles = 2.0 * math.pi / period * product.astype(jnp.float32)
    return (jnp.cos(angles), jnp.sin(angles))


def right_dot(data, table):
    return jnp.dot(data, table, precision=HIGHEST)


def by_columns(first_gate, second_gate, values, filters, skip_gain, grad_output):
    channels, length = filters.shape
    shards = lax.axis_size("ctx")
    blocks = length // shards
    position = lax.axis_index("ctx")
    period = 2 * shards * length
    first = first_gate.astype(jnp.float32)
    second = second_gate.astype(jnp.float32)
    values_wide = values.astype(jnp.float32)
    mixed = first * values_wide
    carried = grad_output.astype(jnp.float32) * second
    signal = jnp.stack([mixed, filters, carried]).reshape(3, channels, blocks, shards)
    spread = lax.all_to_all(signal, "ctx", split_axis=3, concat_axis=3, tiled=True)
    shard_index = jnp.arange(shards, dtype=jnp.int32)
    cosine, sines = turn_table(shard_index, shard_index, 2 * shards)
    parity = (1 - 2 * (shard_index % 2)).astype(jnp.float32)
    fwd_real = jnp.stack([cosine, parity[:, None] * cosine], axis=1)
    fwd_imag = jnp.stack([-sines, -parity[:, None] * sines], axis=1)
    real_part = jnp.einsum("scbm,mjk->scjbk", spread, fwd_real, precision=HIGHEST)
    imag_part = jnp.einsum("scbm,mjk->scjbk", spread, fwd_imag, precision=HIGHEST)
    sectioned = jnp.stack([real_part, imag_part])
    moved = lax.all_to_all(sectioned, "ctx", split_axis=5, concat_axis=5, tiled=True).reshape(
        2, 3, channels, 2, length
    )
    col_real = moved[0]
    col_imag = moved[1]
    col_index = jnp.stack([position, position + shards])
    line_index = jnp.arange(length, dtype=jnp.int32)
    twist_cos, twist_sin = turn_table(col_index, line_index, period)
    turned_real = col_real * twist_cos + col_imag * twist_sin
    turned_imag = col_imag * twist_cos - col_real * twist_sin
    wave_cos, wave_sin = turn_table(line_index, line_index, length)
    spec_real = right_dot(turned_real, wave_cos) + right_dot(turned_imag, wave_sin)
    spec_imag = right_dot(turned_imag, wave_cos) - right_dot(turned_real, wave_sin)
    mixed_real, filter_real, carry_real = (spec_real[0], spec_real[1], spec_real[2])
    mixed_imag, filter_imag, carry_imag = (spec_imag[0], spec_imag[1], spec_imag[2])
    prod_real = jnp.stack(
        [
            filter_real * mixed_real - filter_imag * mixed_imag,
            filter_real * carry_real + filter_imag * carry_imag,
            mixed_real * carry_real + mixed_imag * carry_imag,
        ]
    )
    prod_imag = jnp.stack(
        [
            filter_real * mixed_imag + filter_imag * mixed_real,
            filter_real * carry_imag - filter_imag * carry_real,
            mixed_real * carry_imag - mixed_imag * carry_real,
        ]
    )
    back_real = right_dot(prod_real, wave_cos) - right_dot(prod_imag, wave_sin)
    back_imag = right_dot(prod_real, wave_sin) + right_dot(prod_imag, wave_cos)
    reverted_real = back_real * twist_cos - back_imag * twist_sin
    reverted_imag = back_real * twist_sin + back_imag * twist_cos
    packed = jnp.stack([reverted_real, reverted_imag])
    returned = lax.all_to_all(
        packed.reshape(2, 3, channels, 2, blocks, shards),
        "ctx",
        split_axis=5,
        concat_axis=5,
        tiled=True,
    )
    inv_real = jnp.stack([cosine, cosine * parity[None, :]])
    inv_imag = jnp.stack([-sines, -sines * parity[None, :]])
    timed = jnp.einsum("scjbk,jkm->scbm", returned[0], inv_real, precision=HIGHEST)
    timed = timed + jnp.einsum("scjbk,jkm->scbm", returned[1], inv_imag, precision=HIGHEST)
    timed = timed * (1.0 / period)
    result = lax.all_to_all(timed, "ctx", split_axis=3, concat_axis=3, tiled=True).reshape(
        3, channels, length
    )
    gain = skip_gain[:, None]
    before = result[0] + gain * mixed
    output = second * before
    grad_second = grad_output.astype(jnp.float32) * before
    back_mixed = result[1] + gain * carried
    grad_first = back_mixed * values_wide
    grad_values = back_mixed * first
    grad_filters = result[2]
    grad_skip = lax.psum(jnp.sum(carried * mixed, axis=1), "ctx")
    return (output, grad_first, grad_second, grad_values, grad_filters, grad_skip)


def per_device(first_gate, second_gate, values, filters, skip_gain, grad_output):
    channels, blocks = filters.shape
    shards = lax.axis_size("ctx")
    fits = channels == ROWS * shards and blocks % LANES == 0 and channels <= LANES
    plan = by_channels if fits else by_columns
    return plan(first_gate, second_gate, values, filters, skip_gain, grad_output)


def solution(mesh):
    placed = (
        P("chan", ("groups", "ctx")),
        P("chan", ("groups", "ctx")),
        P("chan", ("groups", "ctx")),
        P("chan", ("groups", "ctx")),
        P("chan"),
        P("chan", ("groups", "ctx")),
    )
    return jax.shard_map(
        per_device,
        mesh=mesh,
        in_specs=placed,
        out_specs=(
            P("chan", ("groups", "ctx")),
            P("chan", ("groups", "ctx")),
            P("chan", ("groups", "ctx")),
            P("chan", ("groups", "ctx")),
            P("chan", ("groups", "ctx")),
            P(("groups", "chan")),
        ),
        check_vma=False,
    )
```

```python
import math

import jax
import jax.numpy as jnp
import numpy as np
from jax import lax
from jax.experimental import pallas as pl
from jax.experimental.pallas import tpu as pltpu
from jax.sharding import PartitionSpec as P

HIGHEST = lax.Precision.HIGHEST
LANES = 128
ROWS = 8
VMEM = pl.BlockSpec(memory_space=pltpu.VMEM)
HBM = pl.BlockSpec(memory_space=pltpu.HBM)
PARAMS = pltpu.CompilerParams(vmem_limit_bytes=48 * 1024 * 1024)


def make_tables(length):
    groups = length // LANES
    period = 2 * length
    turns = 2 * groups
    k1 = np.arange(groups + 1)
    inner = k1[1:-1]
    a = np.arange(groups)
    b = np.arange(LANES)
    cosine = np.cos(2.0 * np.pi / turns * (k1[:, None] * a % turns))
    sine = np.sin(2.0 * np.pi / turns * (inner[:, None] * a % turns))
    weight = np.where((k1 == 0) | (k1 == groups), 1.0, 2.0) / period
    outer = np.concatenate([cosine, sine])
    back = np.concatenate([weight[:, None] * cosine, -2.0 / period * sine]).T
    wave = 2.0 * np.pi / LANES * (b[:, None] * b % LANES)
    twist = 2.0 * np.pi / period * (k1[:, None] * b % period)
    parts = [np.repeat(outer, ROWS, axis=1), np.repeat(back, ROWS, axis=1)]
    parts = [np.concatenate(np.split(part, part.shape[1] // LANES, axis=1)) for part in parts]
    parts += [np.cos(wave), np.sin(wave), np.cos(twist), np.sin(twist)]
    parts.append(np.zeros((-2 * (groups + 1) % ROWS, LANES)))
    return np.concatenate(parts).astype(np.float32)


def spread_rows(table, masked):
    rows, columns = table.shape
    wide = jnp.broadcast_to(table[:, None, :], (rows, ROWS, columns))
    if masked:
        shape = (ROWS, columns)
        own = lax.broadcasted_iota(jnp.int32, shape, 0) == lax.broadcasted_iota(jnp.int32, shape, 1) % ROWS
        wide = jnp.where(own[None], wide, 0.0)
    return wide.reshape(rows * ROWS, columns)


def split(data):
    high = data.astype(jnp.bfloat16)
    return high, (data - high.astype(jnp.float32)).astype(jnp.bfloat16)


def dot(left, right):
    return jnp.dot(left, right, preferred_element_type=jnp.float32)


def long_dot(left, right):
    return dot(left[0], right[0]) + (dot(left[0], right[1]) + dot(left[1], right[0]))


def table_kernel(in_ref, outer_ref, back_ref, forward_ref, inverse_ref, twist_ref):
    groups = outer_ref.shape[2] // ROWS
    tiles = outer_ref.shape[2] // LANES
    row = 0

    def take(rows, pieces=1):
        nonlocal row
        parts = [in_ref[row + i * rows : row + (i + 1) * rows, :] for i in range(pieces)]
        row += rows * pieces
        return jnp.concatenate(parts, axis=1)

    outer_ref[0], outer_ref[1] = split(spread_rows(take(2 * groups, tiles), True))
    back_ref[0], back_ref[1] = split(spread_rows(take(groups, 2 * tiles), True))
    cosine, sine = split(take(LANES)), split(take(LANES))
    for i, (c, s) in enumerate(zip(cosine, sine)):
        forward_ref[i] = jnp.concatenate([jnp.concatenate([c, -s], axis=1), jnp.concatenate([s, c], axis=1)], axis=0)
        inverse_ref[i] = jnp.concatenate([jnp.concatenate([c, s], axis=1), jnp.concatenate([-s, c], axis=1)], axis=0)
    twist_ref[0] = spread_rows(take(groups + 1), False)
    twist_ref[1] = spread_rows(take(groups + 1), False)


def partners(shards):
    far = shards // 2
    return [*range(shards - 1, far - 1, -1), *range(far - 1, -1, -1)] if shards != 8 else [7, 5, 6, 4, 3, 2, 1, 0]


def swap(slabs):
    shards = len(slabs)
    moved = []
    for turn, slab in zip(partners(shards), slabs):
        pairs = [(i, i ^ turn) for i in range(shards)]
        moved.append(lax.ppermute(slab, "ctx", pairs) if turn else slab)
    return moved


def gate_kernel(first_hbm, values_hbm, grad_hbm, second_hbm, filters_hbm, gain_hbm, *refs):
    *out_refs, kept_ref, all_ref, filters_ref, gain_ref, sems = refs
    gates = [kept_ref.at[i] for i in range(4)]
    sources = (first_hbm, values_hbm, filters_hbm, gain_hbm, grad_hbm, second_hbm)
    places = (*gates[:2], filters_ref, gain_ref, *gates[2:])
    copies = [pltpu.make_async_copy(source, place, sems.at[i]) for i, (source, place) in enumerate(zip(sources, places))]
    for copy in copies:
        copy.start()
    shards = len(out_refs)
    channels, blocks = filters_ref.shape
    me = lax.axis_index("ctx")

    def place(s, signal):
        for j in range(blocks // LANES):
            tile = signal[:, j * LANES : (j + 1) * LANES].reshape(shards, ROWS, LANES)
            all_ref[:, s, :, j * LANES : (j + 1) * LANES] = tile

    copies[0].wait()
    copies[1].wait()
    place(0, kept_ref[0].astype(jnp.float32) * kept_ref[1].astype(jnp.float32))
    copies[2].wait()
    copies[3].wait()
    shape = (channels, channels)
    diagonal = lax.broadcasted_iota(jnp.int32, shape, 0) == lax.broadcasted_iota(jnp.int32, shape, 1)
    gain = jnp.sum(jnp.where(diagonal, gain_ref[...], 0.0), axis=1, keepdims=True)
    position = me * blocks + lax.broadcasted_iota(jnp.int32, (channels, blocks), 1)
    place(1, filters_ref[...] + jnp.where(position == 0, gain, 0.0))
    copies[4].wait()
    copies[5].wait()
    place(2, kept_ref[2].astype(jnp.float32) * kept_ref[3].astype(jnp.float32))
    for turn, out_ref in zip(partners(shards), out_refs):
        out_ref[...] = all_ref[me ^ turn]


def spectral_kernel(outer_ref, back_ref, forward_ref, inverse_ref, twist_ref, *refs):
    *refs, all_ref, in_ref = refs
    shards = len(refs) // 2
    in_refs, out_refs = refs[:shards], refs[shards:]
    me = lax.axis_index("ctx")
    for turn, ref in zip(partners(shards), in_refs):
        in_ref[me ^ turn] = ref[...]
    tiles = in_ref.shape[3] // LANES
    span = tiles * ROWS
    rows = shards * span
    spec_rows = rows + ROWS
    cosine, sine = twist_ref[0], twist_ref[1]

    def take(s):
        parts = [in_ref[:, s, :, j * LANES : (j + 1) * LANES] for j in range(tiles)]
        return jnp.stack(parts, axis=1).reshape(rows, LANES)

    signals = [take(s) for s in range(3)]
    total = jnp.sum((signals[0] * signals[2]).reshape(rows // ROWS, ROWS, LANES), axis=0)
    total = jnp.broadcast_to(jnp.sum(total, axis=1, keepdims=True), (ROWS, LANES))
    all_ref[:, 3 * span :, :] = jnp.broadcast_to(total[None], (shards, ROWS, LANES))
    columns = long_dot(outer_ref, split(jnp.concatenate(signals, axis=1)))
    edge = jnp.zeros((ROWS, LANES), jnp.float32)
    spectra = []
    for s in range(3):
        lanes = slice(s * LANES, (s + 1) * LANES)
        real = columns[:spec_rows, lanes]
        imag = jnp.concatenate([edge, columns[spec_rows:, lanes], edge], axis=0)
        turned = jnp.concatenate([real * cosine - imag * sine, -(real * sine + imag * cosine)], axis=1)
        spectra.append(long_dot(split(turned), forward_ref))
    (mr, mi), (fr, fi), (cr, ci) = [(x[:, :LANES], x[:, LANES:]) for x in spectra]
    products = (
        (fr * mr - fi * mi, fr * mi + fi * mr),
        (fr * cr + fi * ci, fr * ci - fi * cr),
        (mr * cr + mi * ci, mr * ci - mi * cr),
    )
    reverted = []
    for real, imag in products:
        waves = long_dot(split(jnp.concatenate([real, imag], axis=1)), inverse_ref)
        real, imag = waves[:, :LANES], waves[:, LANES:]
        turned_imag = real * sine + imag * cosine
        reverted.append(jnp.concatenate([real * cosine - imag * sine, turned_imag[ROWS:-ROWS]], axis=0))
    result = long_dot(back_ref, split(jnp.concatenate(reverted, axis=1)))
    for s in range(3):
        all_ref[:, s * span : (s + 1) * span, :] = result[:, s * LANES : (s + 1) * LANES].reshape(shards, span, LANES)
    for turn, out_ref in zip(partners(shards), out_refs):
        out_ref[...] = all_ref[me ^ turn]


def output_kernel(kept_ref, *refs):
    _, channels, blocks = kept_ref.shape
    tiles = blocks // LANES
    shards = channels // ROWS
    in_refs, (out_ref, gfirst_ref, gsecond_ref, gvalues_ref, gfilters_ref, gskip_ref, result_ref, total_ref) = refs[:shards], refs[shards:]
    me = lax.axis_index("ctx")
    for turn, in_ref in zip(partners(shards), in_refs):
        own = pl.ds(pl.multiple_of((me ^ turn) * ROWS, ROWS), ROWS)
        for s, dst_ref in enumerate((result_ref.at[0], result_ref.at[1], gfilters_ref)):
            for j in range(tiles):
                dst_ref[own, j * LANES : (j + 1) * LANES] = in_ref[(s * tiles + j) * ROWS : (s * tiles + j + 1) * ROWS, :]
        total_ref[own, :] = in_ref[3 * tiles * ROWS :, :]
    first, values, grad, second = [kept_ref[i].astype(jnp.float32) for i in range(4)]
    before = result_ref[0]
    out_ref[...] = second * before
    gsecond_ref[...] = grad * before
    back = result_ref[1]
    gfirst_ref[...] = back * values
    gvalues_ref[...] = back * first
    shape = (channels, channels)
    diagonal = lax.broadcasted_iota(jnp.int32, shape, 0) == lax.broadcasted_iota(jnp.int32, shape, 1)
    gskip_ref[...] = jnp.sum(jnp.where(diagonal, total_ref[:, :channels], 0.0), axis=0, keepdims=True)


def call(kernel, out_shape, args, scratch_shapes=()):
    return pl.pallas_call(
        kernel,
        out_shape=out_shape,
        in_specs=[VMEM] * len(args),
        out_specs=[VMEM] * len(out_shape),
        scratch_shapes=scratch_shapes,
        compiler_params=PARAMS,
    )(*args)


def by_channels(first_gate, second_gate, values, filters, skip_gain, grad_output):
    channels, blocks = filters.shape
    shards = lax.axis_size("ctx")
    tiles = blocks // LANES
    length = blocks * shards
    rows = length // LANES * ROWS
    wide, half = jnp.float32, jnp.bfloat16
    sources = (first_gate, values, grad_output, second_gate, filters, skip_gain.reshape(1, channels))
    *slabs, kept = pl.pallas_call(
        gate_kernel,
        out_shape=[pltpu.VMEM((3, ROWS, blocks), wide)] * shards + [pltpu.VMEM((4, channels, blocks), half)],
        in_specs=[HBM] * len(sources),
        out_specs=[VMEM] * (shards + 1),
        scratch_shapes=[
            pltpu.VMEM((shards, 3, ROWS, blocks), wide),
            pltpu.VMEM((channels, blocks), wide),
            pltpu.VMEM((1, channels), wide),
            pltpu.SemaphoreType.DMA((len(sources),)),
        ],
        compiler_params=PARAMS,
    )(*[pltpu.with_memory_space_constraint(source, pltpu.HBM) for source in sources])
    tables = call(
        table_kernel,
        [
            pltpu.VMEM((2, 2 * rows, rows), half),
            pltpu.VMEM((2, rows, 2 * rows), half),
            pltpu.VMEM((2, 2 * LANES, 2 * LANES), half),
            pltpu.VMEM((2, 2 * LANES, 2 * LANES), half),
            pltpu.VMEM((2, rows + ROWS, LANES), wide),
        ],
        [jnp.asarray(make_tables(length))],
    )
    slab = ((3 * tiles + 1) * ROWS, LANES)
    slabs = call(
        spectral_kernel,
        [pltpu.VMEM(slab, wide)] * shards,
        (*tables, *swap(slabs)),
        [pltpu.VMEM((shards, *slab), wide), pltpu.VMEM((shards, 3, ROWS, blocks), wide)],
    )
    *full, grad_skip = call(
        output_kernel,
        [jax.ShapeDtypeStruct((channels, blocks), wide)] * 5 + [jax.ShapeDtypeStruct((1, channels), wide)],
        (kept, *swap(slabs)),
        [pltpu.VMEM((2, channels, blocks), wide), pltpu.VMEM((channels, LANES), wide)],
    )
    return (*full, grad_skip.reshape(channels))


def turn_table(first_index, second_index, period):
    product = first_index[:, None] * second_index[None, :] % period
    angles = 2.0 * math.pi / period * product.astype(jnp.float32)
    return (jnp.cos(angles), jnp.sin(angles))


def right_dot(data, table):
    return jnp.dot(data, table, precision=HIGHEST)


def by_columns(first_gate, second_gate, values, filters, skip_gain, grad_output):
    channels, length = filters.shape
    shards = lax.axis_size("ctx")
    blocks = length // shards
    position = lax.axis_index("ctx")
    period = 2 * shards * length
    first = first_gate.astype(jnp.float32)
    second = second_gate.astype(jnp.float32)
    values_wide = values.astype(jnp.float32)
    mixed = first * values_wide
    carried = grad_output.astype(jnp.float32) * second
    signal = jnp.stack([mixed, filters, carried]).reshape(3, channels, blocks, shards)
    spread = lax.all_to_all(signal, "ctx", split_axis=3, concat_axis=3, tiled=True)
    shard_index = jnp.arange(shards, dtype=jnp.int32)
    cosine, sines = turn_table(shard_index, shard_index, 2 * shards)
    parity = (1 - 2 * (shard_index % 2)).astype(jnp.float32)
    fwd_real = jnp.stack([cosine, parity[:, None] * cosine], axis=1)
    fwd_imag = jnp.stack([-sines, -parity[:, None] * sines], axis=1)
    real_part = jnp.einsum("scbm,mjk->scjbk", spread, fwd_real, precision=HIGHEST)
    imag_part = jnp.einsum("scbm,mjk->scjbk", spread, fwd_imag, precision=HIGHEST)
    sectioned = jnp.stack([real_part, imag_part])
    moved = lax.all_to_all(sectioned, "ctx", split_axis=5, concat_axis=5, tiled=True).reshape(
        2, 3, channels, 2, length
    )
    col_real = moved[0]
    col_imag = moved[1]
    col_index = jnp.stack([position, position + shards])
    line_index = jnp.arange(length, dtype=jnp.int32)
    twist_cos, twist_sin = turn_table(col_index, line_index, period)
    turned_real = col_real * twist_cos + col_imag * twist_sin
    turned_imag = col_imag * twist_cos - col_real * twist_sin
    wave_cos, wave_sin = turn_table(line_index, line_index, length)
    spec_real = right_dot(turned_real, wave_cos) + right_dot(turned_imag, wave_sin)
    spec_imag = right_dot(turned_imag, wave_cos) - right_dot(turned_real, wave_sin)
    mixed_real, filter_real, carry_real = (spec_real[0], spec_real[1], spec_real[2])
    mixed_imag, filter_imag, carry_imag = (spec_imag[0], spec_imag[1], spec_imag[2])
    prod_real = jnp.stack(
        [
            filter_real * mixed_real - filter_imag * mixed_imag,
            filter_real * carry_real + filter_imag * carry_imag,
            mixed_real * carry_real + mixed_imag * carry_imag,
        ]
    )
    prod_imag = jnp.stack(
        [
            filter_real * mixed_imag + filter_imag * mixed_real,
            filter_real * carry_imag - filter_imag * carry_real,
            mixed_real * carry_imag - mixed_imag * carry_real,
        ]
    )
    back_real = right_dot(prod_real, wave_cos) - right_dot(prod_imag, wave_sin)
    back_imag = right_dot(prod_real, wave_sin) + right_dot(prod_imag, wave_cos)
    reverted_real = back_real * twist_cos - back_imag * twist_sin
    reverted_imag = back_real * twist_sin + back_imag * twist_cos
    packed = jnp.stack([reverted_real, reverted_imag])
    returned = lax.all_to_all(
        packed.reshape(2, 3, channels, 2, blocks, shards),
        "ctx",
        split_axis=5,
        concat_axis=5,
        tiled=True,
    )
    inv_real = jnp.stack([cosine, cosine * parity[None, :]])
    inv_imag = jnp.stack([-sines, -sines * parity[None, :]])
    timed = jnp.einsum("scjbk,jkm->scbm", returned[0], inv_real, precision=HIGHEST)
    timed = timed + jnp.einsum("scjbk,jkm->scbm", returned[1], inv_imag, precision=HIGHEST)
    timed = timed * (1.0 / period)
    result = lax.all_to_all(timed, "ctx", split_axis=3, concat_axis=3, tiled=True).reshape(
        3, channels, length
    )
    gain = skip_gain[:, None]
    before = result[0] + gain * mixed
    output = second * before
    grad_second = grad_output.astype(jnp.float32) * before
    back_mixed = result[1] + gain * carried
    grad_first = back_mixed * values_wide
    grad_values = back_mixed * first
    grad_filters = result[2]
    grad_skip = lax.psum(jnp.sum(carried * mixed, axis=1), "ctx")
    return (output, grad_first, grad_second, grad_values, grad_filters, grad_skip)


def per_device(first_gate, second_gate, values, filters, skip_gain, grad_output):
    channels, blocks = filters.shape
    shards = lax.axis_size("ctx")
    fits = channels == ROWS * shards and blocks % LANES == 0 and channels <= LANES
    plan = by_channels if fits else by_columns
    return plan(first_gate, second_gate, values, filters, skip_gain, grad_output)


def solution(mesh):
    placed = (
        P("chan", ("groups", "ctx")),
        P("chan", ("groups", "ctx")),
        P("chan", ("groups", "ctx")),
        P("chan", ("groups", "ctx")),
        P("chan"),
        P("chan", ("groups", "ctx")),
    )
    return jax.shard_map(
        per_device,
        mesh=mesh,
        in_specs=placed,
        out_specs=(
            P("chan", ("groups", "ctx")),
            P("chan", ("groups", "ctx")),
            P("chan", ("groups", "ctx")),
            P("chan", ("groups", "ctx")),
            P("chan", ("groups", "ctx")),
            P(("groups", "chan")),
        ),
        check_vma=False,
    )
```

```python
import math

import jax
import jax.numpy as jnp
import numpy as np
from jax import lax
from jax.experimental import pallas as pl
from jax.experimental.pallas import tpu as pltpu
from jax.sharding import PartitionSpec as P

HIGHEST = lax.Precision.HIGHEST
OUTWARD = (4, 7, 3, 5, 6, 2, 1, 0)
HOMEWARD = (7, 3, 6, 5, 4, 2, 1, 0)
LANES = 128
ROWS = 8
VMEM = pl.BlockSpec(memory_space=pltpu.VMEM)
HBM = pl.BlockSpec(memory_space=pltpu.HBM)
PARAMS = pltpu.CompilerParams(vmem_limit_bytes=48 * 1024 * 1024)


def make_tables(length):
    groups = length // LANES
    period = 2 * length
    turns = 2 * groups
    k1 = np.arange(groups + 1)
    inner = k1[1:-1]
    a = np.arange(groups)
    b = np.arange(LANES)
    cosine = np.cos(2.0 * np.pi / turns * (k1[:, None] * a % turns))
    sine = np.sin(2.0 * np.pi / turns * (inner[:, None] * a % turns))
    weight = np.where((k1 == 0) | (k1 == groups), 1.0, 2.0) / period
    outer = np.concatenate([cosine, sine])
    back = np.concatenate([weight[:, None] * cosine, -2.0 / period * sine]).T
    wave = 2.0 * np.pi / LANES * (b[:, None] * b % LANES)
    twist = 2.0 * np.pi / period * (k1[:, None] * b % period)
    parts = [np.repeat(outer, ROWS, axis=1), np.repeat(back, ROWS, axis=1)]
    parts = [np.concatenate(np.split(part, part.shape[1] // LANES, axis=1)) for part in parts]
    parts += [np.cos(wave), np.sin(wave), np.cos(twist), np.sin(twist)]
    parts.append(np.zeros((-2 * (groups + 1) % ROWS, LANES)))
    return np.concatenate(parts).astype(np.float32)


def spread_rows(table, masked):
    rows, columns = table.shape
    wide = jnp.broadcast_to(table[:, None, :], (rows, ROWS, columns))
    if masked:
        shape = (ROWS, columns)
        own = lax.broadcasted_iota(jnp.int32, shape, 0) == lax.broadcasted_iota(jnp.int32, shape, 1) % ROWS
        wide = jnp.where(own[None], wide, 0.0)
    return wide.reshape(rows * ROWS, columns)


def split(data):
    high = data.astype(jnp.bfloat16)
    return high, (data - high.astype(jnp.float32)).astype(jnp.bfloat16)


def dot(left, right):
    return jnp.dot(left, right, preferred_element_type=jnp.float32)


def long_dot(left, right):
    return dot(left[0], right[0]) + (dot(left[0], right[1]) + dot(left[1], right[0]))


def table_kernel(in_ref, outer_ref, back_ref, forward_ref, inverse_ref, twist_ref):
    groups = outer_ref.shape[2] // ROWS
    tiles = outer_ref.shape[2] // LANES
    row = 0

    def take(rows, pieces=1):
        nonlocal row
        parts = [in_ref[row + i * rows : row + (i + 1) * rows, :] for i in range(pieces)]
        row += rows * pieces
        return jnp.concatenate(parts, axis=1)

    outer_ref[0], outer_ref[1] = split(spread_rows(take(2 * groups, tiles), True))
    back_ref[0], back_ref[1] = split(spread_rows(take(groups, 2 * tiles), True))
    cosine, sine = split(take(LANES)), split(take(LANES))
    for i, (c, s) in enumerate(zip(cosine, sine)):
        forward_ref[i] = jnp.concatenate([jnp.concatenate([c, -s], axis=1), jnp.concatenate([s, c], axis=1)], axis=0)
        inverse_ref[i] = jnp.concatenate([jnp.concatenate([c, s], axis=1), jnp.concatenate([-s, c], axis=1)], axis=0)
    twist_ref[0] = spread_rows(take(groups + 1), False)
    twist_ref[1] = spread_rows(take(groups + 1), False)


def turns(shards, order):
    return order if len(order) == shards else tuple(range(shards - 1, -1, -1))


def swap(slabs, order):
    moved = []
    for turn, slab in zip(order, slabs):
        pairs = [(i, i ^ turn) for i in range(len(slabs))]
        moved.append(lax.ppermute(slab, "ctx", pairs) if turn else slab)
    return moved


def gate_kernel(first_hbm, values_hbm, grad_hbm, second_hbm, filters_hbm, gain_hbm, *refs):
    *out_refs, kept_ref, all_ref, filters_ref, gain_ref, sems = refs
    gates = [kept_ref.at[i] for i in range(4)]
    sources = (first_hbm, values_hbm, filters_hbm, gain_hbm, grad_hbm, second_hbm)
    places = (*gates[:2], filters_ref, gain_ref, *gates[2:])
    copies = [pltpu.make_async_copy(source, place, sems.at[i]) for i, (source, place) in enumerate(zip(sources, places))]
    for copy in copies:
        copy.start()
    shards = len(out_refs)
    channels, blocks = filters_ref.shape
    me = lax.axis_index("ctx")

    def place(s, signal):
        for j in range(blocks // LANES):
            tile = signal[:, j * LANES : (j + 1) * LANES].reshape(shards, ROWS, LANES)
            all_ref[:, s, :, j * LANES : (j + 1) * LANES] = tile

    copies[0].wait()
    copies[1].wait()
    place(0, kept_ref[0].astype(jnp.float32) * kept_ref[1].astype(jnp.float32))
    copies[2].wait()
    copies[3].wait()
    shape = (channels, channels)
    diagonal = lax.broadcasted_iota(jnp.int32, shape, 0) == lax.broadcasted_iota(jnp.int32, shape, 1)
    gain = jnp.sum(jnp.where(diagonal, gain_ref[...], 0.0), axis=1, keepdims=True)
    position = me * blocks + lax.broadcasted_iota(jnp.int32, (channels, blocks), 1)
    place(1, filters_ref[...] + jnp.where(position == 0, gain, 0.0))
    copies[4].wait()
    copies[5].wait()
    place(2, kept_ref[2].astype(jnp.float32) * kept_ref[3].astype(jnp.float32))
    for turn, out_ref in zip(turns(shards, OUTWARD), out_refs):
        out_ref[...] = all_ref[me ^ turn]


def spectral_kernel(outer_ref, back_ref, forward_ref, inverse_ref, twist_ref, *refs):
    *refs, all_ref, in_ref = refs
    shards = len(refs) // 2
    in_refs, out_refs = refs[:shards], refs[shards:]
    me = lax.axis_index("ctx")
    for turn, ref in zip(turns(shards, OUTWARD), in_refs):
        in_ref[me ^ turn] = ref[...]
    tiles = in_ref.shape[3] // LANES
    span = tiles * ROWS
    rows = shards * span
    spec_rows = rows + ROWS
    cosine, sine = twist_ref[0], twist_ref[1]

    def take(s):
        parts = [in_ref[:, s, :, j * LANES : (j + 1) * LANES] for j in range(tiles)]
        return jnp.stack(parts, axis=1).reshape(rows, LANES)

    signals = [take(s) for s in range(3)]
    total = jnp.sum((signals[0] * signals[2]).reshape(rows // ROWS, ROWS, LANES), axis=0)
    total = jnp.broadcast_to(jnp.sum(total, axis=1, keepdims=True), (ROWS, LANES))
    all_ref[:, 3 * span :, :] = jnp.broadcast_to(total[None], (shards, ROWS, LANES))
    columns = long_dot(outer_ref, split(jnp.concatenate(signals, axis=1)))
    edge = jnp.zeros((ROWS, LANES), jnp.float32)
    spectra = []
    for s in range(3):
        lanes = slice(s * LANES, (s + 1) * LANES)
        real = columns[:spec_rows, lanes]
        imag = jnp.concatenate([edge, columns[spec_rows:, lanes], edge], axis=0)
        turned = jnp.concatenate([real * cosine - imag * sine, -(real * sine + imag * cosine)], axis=1)
        spectra.append(long_dot(split(turned), forward_ref))
    (mr, mi), (fr, fi), (cr, ci) = [(x[:, :LANES], x[:, LANES:]) for x in spectra]
    products = (
        (fr * mr - fi * mi, fr * mi + fi * mr),
        (fr * cr + fi * ci, fr * ci - fi * cr),
        (mr * cr + mi * ci, mr * ci - mi * cr),
    )
    reverted = []
    for real, imag in products:
        waves = long_dot(split(jnp.concatenate([real, imag], axis=1)), inverse_ref)
        real, imag = waves[:, :LANES], waves[:, LANES:]
        turned_imag = real * sine + imag * cosine
        reverted.append(jnp.concatenate([real * cosine - imag * sine, turned_imag[ROWS:-ROWS]], axis=0))
    result = long_dot(back_ref, split(jnp.concatenate(reverted, axis=1)))
    for s in range(3):
        all_ref[:, s * span : (s + 1) * span, :] = result[:, s * LANES : (s + 1) * LANES].reshape(shards, span, LANES)
    for turn, out_ref in zip(turns(shards, HOMEWARD), out_refs):
        out_ref[...] = all_ref[me ^ turn]


def output_kernel(kept_ref, *refs):
    _, channels, blocks = kept_ref.shape
    tiles = blocks // LANES
    shards = channels // ROWS
    in_refs, (out_ref, gfirst_ref, gsecond_ref, gvalues_ref, gfilters_ref, gskip_ref, result_ref, total_ref) = refs[:shards], refs[shards:]
    me = lax.axis_index("ctx")
    for turn, in_ref in zip(turns(shards, HOMEWARD), in_refs):
        own = pl.ds(pl.multiple_of((me ^ turn) * ROWS, ROWS), ROWS)
        for s, dst_ref in enumerate((result_ref.at[0], result_ref.at[1], gfilters_ref)):
            for j in range(tiles):
                dst_ref[own, j * LANES : (j + 1) * LANES] = in_ref[(s * tiles + j) * ROWS : (s * tiles + j + 1) * ROWS, :]
        total_ref[own, :] = in_ref[3 * tiles * ROWS :, :]
    first, values, grad, second = [kept_ref[i].astype(jnp.float32) for i in range(4)]
    before = result_ref[0]
    out_ref[...] = second * before
    gsecond_ref[...] = grad * before
    back = result_ref[1]
    gfirst_ref[...] = back * values
    gvalues_ref[...] = back * first
    shape = (channels, channels)
    diagonal = lax.broadcasted_iota(jnp.int32, shape, 0) == lax.broadcasted_iota(jnp.int32, shape, 1)
    gskip_ref[...] = jnp.sum(jnp.where(diagonal, total_ref[:, :channels], 0.0), axis=0, keepdims=True)


def call(kernel, out_shape, args, scratch_shapes=()):
    return pl.pallas_call(
        kernel,
        out_shape=out_shape,
        in_specs=[VMEM] * len(args),
        out_specs=[VMEM] * len(out_shape),
        scratch_shapes=scratch_shapes,
        compiler_params=PARAMS,
    )(*args)


def by_channels(first_gate, second_gate, values, filters, skip_gain, grad_output):
    channels, blocks = filters.shape
    shards = lax.axis_size("ctx")
    tiles = blocks // LANES
    length = blocks * shards
    rows = length // LANES * ROWS
    wide, half = jnp.float32, jnp.bfloat16
    sources = (first_gate, values, grad_output, second_gate, filters, skip_gain.reshape(1, channels))
    *slabs, kept = pl.pallas_call(
        gate_kernel,
        out_shape=[pltpu.VMEM((3, ROWS, blocks), wide)] * shards + [pltpu.VMEM((4, channels, blocks), half)],
        in_specs=[HBM] * len(sources),
        out_specs=[VMEM] * (shards + 1),
        scratch_shapes=[
            pltpu.VMEM((shards, 3, ROWS, blocks), wide),
            pltpu.VMEM((channels, blocks), wide),
            pltpu.VMEM((1, channels), wide),
            pltpu.SemaphoreType.DMA((len(sources),)),
        ],
        compiler_params=PARAMS,
    )(*[pltpu.with_memory_space_constraint(source, pltpu.HBM) for source in sources])
    tables = call(
        table_kernel,
        [
            pltpu.VMEM((2, 2 * rows, rows), half),
            pltpu.VMEM((2, rows, 2 * rows), half),
            pltpu.VMEM((2, 2 * LANES, 2 * LANES), half),
            pltpu.VMEM((2, 2 * LANES, 2 * LANES), half),
            pltpu.VMEM((2, rows + ROWS, LANES), wide),
        ],
        [jnp.asarray(make_tables(length))],
    )
    slab = ((3 * tiles + 1) * ROWS, LANES)
    slabs = call(
        spectral_kernel,
        [pltpu.VMEM(slab, wide)] * shards,
        (*tables, *swap(slabs, turns(shards, OUTWARD))),
        [pltpu.VMEM((shards, *slab), wide), pltpu.VMEM((shards, 3, ROWS, blocks), wide)],
    )
    *full, grad_skip = call(
        output_kernel,
        [jax.ShapeDtypeStruct((channels, blocks), wide)] * 5 + [jax.ShapeDtypeStruct((1, channels), wide)],
        (kept, *swap(slabs, turns(shards, HOMEWARD))),
        [pltpu.VMEM((2, channels, blocks), wide), pltpu.VMEM((channels, LANES), wide)],
    )
    return (*full, grad_skip.reshape(channels))


def turn_table(first_index, second_index, period):
    product = first_index[:, None] * second_index[None, :] % period
    angles = 2.0 * math.pi / period * product.astype(jnp.float32)
    return (jnp.cos(angles), jnp.sin(angles))


def right_dot(data, table):
    return jnp.dot(data, table, precision=HIGHEST)


def by_columns(first_gate, second_gate, values, filters, skip_gain, grad_output):
    channels, length = filters.shape
    shards = lax.axis_size("ctx")
    blocks = length // shards
    position = lax.axis_index("ctx")
    period = 2 * shards * length
    first = first_gate.astype(jnp.float32)
    second = second_gate.astype(jnp.float32)
    values_wide = values.astype(jnp.float32)
    mixed = first * values_wide
    carried = grad_output.astype(jnp.float32) * second
    signal = jnp.stack([mixed, filters, carried]).reshape(3, channels, blocks, shards)
    spread = lax.all_to_all(signal, "ctx", split_axis=3, concat_axis=3, tiled=True)
    shard_index = jnp.arange(shards, dtype=jnp.int32)
    cosine, sines = turn_table(shard_index, shard_index, 2 * shards)
    parity = (1 - 2 * (shard_index % 2)).astype(jnp.float32)
    fwd_real = jnp.stack([cosine, parity[:, None] * cosine], axis=1)
    fwd_imag = jnp.stack([-sines, -parity[:, None] * sines], axis=1)
    real_part = jnp.einsum("scbm,mjk->scjbk", spread, fwd_real, precision=HIGHEST)
    imag_part = jnp.einsum("scbm,mjk->scjbk", spread, fwd_imag, precision=HIGHEST)
    sectioned = jnp.stack([real_part, imag_part])
    moved = lax.all_to_all(sectioned, "ctx", split_axis=5, concat_axis=5, tiled=True).reshape(
        2, 3, channels, 2, length
    )
    col_real = moved[0]
    col_imag = moved[1]
    col_index = jnp.stack([position, position + shards])
    line_index = jnp.arange(length, dtype=jnp.int32)
    twist_cos, twist_sin = turn_table(col_index, line_index, period)
    turned_real = col_real * twist_cos + col_imag * twist_sin
    turned_imag = col_imag * twist_cos - col_real * twist_sin
    wave_cos, wave_sin = turn_table(line_index, line_index, length)
    spec_real = right_dot(turned_real, wave_cos) + right_dot(turned_imag, wave_sin)
    spec_imag = right_dot(turned_imag, wave_cos) - right_dot(turned_real, wave_sin)
    mixed_real, filter_real, carry_real = (spec_real[0], spec_real[1], spec_real[2])
    mixed_imag, filter_imag, carry_imag = (spec_imag[0], spec_imag[1], spec_imag[2])
    prod_real = jnp.stack(
        [
            filter_real * mixed_real - filter_imag * mixed_imag,
            filter_real * carry_real + filter_imag * carry_imag,
            mixed_real * carry_real + mixed_imag * carry_imag,
        ]
    )
    prod_imag = jnp.stack(
        [
            filter_real * mixed_imag + filter_imag * mixed_real,
            filter_real * carry_imag - filter_imag * carry_real,
            mixed_real * carry_imag - mixed_imag * carry_real,
        ]
    )
    back_real = right_dot(prod_real, wave_cos) - right_dot(prod_imag, wave_sin)
    back_imag = right_dot(prod_real, wave_sin) + right_dot(prod_imag, wave_cos)
    reverted_real = back_real * twist_cos - back_imag * twist_sin
    reverted_imag = back_real * twist_sin + back_imag * twist_cos
    packed = jnp.stack([reverted_real, reverted_imag])
    returned = lax.all_to_all(
        packed.reshape(2, 3, channels, 2, blocks, shards),
        "ctx",
        split_axis=5,
        concat_axis=5,
        tiled=True,
    )
    inv_real = jnp.stack([cosine, cosine * parity[None, :]])
    inv_imag = jnp.stack([-sines, -sines * parity[None, :]])
    timed = jnp.einsum("scjbk,jkm->scbm", returned[0], inv_real, precision=HIGHEST)
    timed = timed + jnp.einsum("scjbk,jkm->scbm", returned[1], inv_imag, precision=HIGHEST)
    timed = timed * (1.0 / period)
    result = lax.all_to_all(timed, "ctx", split_axis=3, concat_axis=3, tiled=True).reshape(
        3, channels, length
    )
    gain = skip_gain[:, None]
    before = result[0] + gain * mixed
    output = second * before
    grad_second = grad_output.astype(jnp.float32) * before
    back_mixed = result[1] + gain * carried
    grad_first = back_mixed * values_wide
    grad_values = back_mixed * first
    grad_filters = result[2]
    grad_skip = lax.psum(jnp.sum(carried * mixed, axis=1), "ctx")
    return (output, grad_first, grad_second, grad_values, grad_filters, grad_skip)


def per_device(first_gate, second_gate, values, filters, skip_gain, grad_output):
    channels, blocks = filters.shape
    shards = lax.axis_size("ctx")
    fits = channels == ROWS * shards and shards & (shards - 1) == 0 and blocks % LANES == 0 and channels <= LANES
    plan = by_channels if fits else by_columns
    return plan(first_gate, second_gate, values, filters, skip_gain, grad_output)


def solution(mesh):
    placed = (
        P("chan", ("groups", "ctx")),
        P("chan", ("groups", "ctx")),
        P("chan", ("groups", "ctx")),
        P("chan", ("groups", "ctx")),
        P("chan"),
        P("chan", ("groups", "ctx")),
    )
    return jax.shard_map(
        per_device,
        mesh=mesh,
        in_specs=placed,
        out_specs=(
            P("chan", ("groups", "ctx")),
            P("chan", ("groups", "ctx")),
            P("chan", ("groups", "ctx")),
            P("chan", ("groups", "ctx")),
            P("chan", ("groups", "ctx")),
            P(("groups", "chan")),
        ),
        check_vma=False,
    )
```

```python
import math

import jax
import jax.numpy as jnp
import numpy as np
from jax import lax
from jax.experimental import pallas as pl
from jax.experimental.pallas import tpu as pltpu
from jax.sharding import PartitionSpec as P

HIGHEST = lax.Precision.HIGHEST
OUTWARD = ((6, 7), (2, 3), (5,), (1,), (4,))
HOMEWARD = ((6, 7), (2, 3), (1,), (5,), (4,))
LANES = 128
ROWS = 8
VMEM = pl.BlockSpec(memory_space=pltpu.VMEM)
HBM = pl.BlockSpec(memory_space=pltpu.HBM)
PARAMS = pltpu.CompilerParams(vmem_limit_bytes=48 * 1024 * 1024)


def make_tables(length):
    groups = length // LANES
    period = 2 * length
    turns = 2 * groups
    k1 = np.arange(groups + 1)
    inner = k1[1:-1]
    a = np.arange(groups)
    b = np.arange(LANES)
    cosine = np.cos(2.0 * np.pi / turns * (k1[:, None] * a % turns))
    sine = np.sin(2.0 * np.pi / turns * (inner[:, None] * a % turns))
    weight = np.where((k1 == 0) | (k1 == groups), 1.0, 2.0) / period
    outer = np.concatenate([cosine, sine])
    back = np.concatenate([weight[:, None] * cosine, -2.0 / period * sine]).T
    wave = 2.0 * np.pi / LANES * (b[:, None] * b % LANES)
    twist = 2.0 * np.pi / period * (k1[:, None] * b % period)
    parts = [np.repeat(outer, ROWS, axis=1), np.repeat(back, ROWS, axis=1)]
    parts = [np.concatenate(np.split(part, part.shape[1] // LANES, axis=1)) for part in parts]
    parts += [np.cos(wave), np.sin(wave), np.cos(twist), np.sin(twist)]
    parts.append(np.zeros((-2 * (groups + 1) % ROWS, LANES)))
    return np.concatenate(parts).astype(np.float32)


def spread_rows(table, masked):
    rows, columns = table.shape
    wide = jnp.broadcast_to(table[:, None, :], (rows, ROWS, columns))
    if masked:
        shape = (ROWS, columns)
        own = lax.broadcasted_iota(jnp.int32, shape, 0) == lax.broadcasted_iota(jnp.int32, shape, 1) % ROWS
        wide = jnp.where(own[None], wide, 0.0)
    return wide.reshape(rows * ROWS, columns)


def split(data):
    high = data.astype(jnp.bfloat16)
    return high, (data - high.astype(jnp.float32)).astype(jnp.bfloat16)


def dot(left, right):
    return jnp.dot(left, right, preferred_element_type=jnp.float32)


def long_dot(left, right):
    return dot(left[0], right[0]) + (dot(left[0], right[1]) + dot(left[1], right[0]))


def table_kernel(in_ref, outer_ref, back_ref, forward_ref, inverse_ref, twist_ref):
    groups = outer_ref.shape[2] // ROWS
    tiles = outer_ref.shape[2] // LANES
    row = 0

    def take(rows, pieces=1):
        nonlocal row
        parts = [in_ref[row + i * rows : row + (i + 1) * rows, :] for i in range(pieces)]
        row += rows * pieces
        return jnp.concatenate(parts, axis=1)

    outer_ref[0], outer_ref[1] = split(spread_rows(take(2 * groups, tiles), True))
    back_ref[0], back_ref[1] = split(spread_rows(take(groups, 2 * tiles), True))
    cosine, sine = split(take(LANES)), split(take(LANES))
    for i, (c, s) in enumerate(zip(cosine, sine)):
        forward_ref[i] = jnp.concatenate([jnp.concatenate([c, -s], axis=1), jnp.concatenate([s, c], axis=1)], axis=0)
        inverse_ref[i] = jnp.concatenate([jnp.concatenate([c, s], axis=1), jnp.concatenate([-s, c], axis=1)], axis=0)
    twist_ref[0] = spread_rows(take(groups + 1), False)
    twist_ref[1] = spread_rows(take(groups + 1), False)


def sent(shards, groups):
    if sum(map(len, groups)) != shards - 1:
        groups = tuple((turn,) for turn in range(shards - 1, 0, -1))
    return (*groups, (0,))


def received(shards, groups):
    groups = sent(shards, groups)
    first = [(group[0], *(None for _ in group[1:])) for group in groups]
    return (*first[:-1], *(group[1:] for group in groups if len(group) > 1), (0,))


def swap(arrays, groups):
    *arrays, own = arrays
    shards = lax.axis_size("ctx")

    def move(array, turn):
        return lax.ppermute(array, "ctx", [(i, i ^ turn) for i in range(shards)])

    moved = [move(x, members[0]) for members, x in zip(sent(shards, groups), arrays)]
    relayed = [move(x[1:], 1) for x in moved if x.shape[0] > 1]
    return (*moved, *relayed, own)


def gather(place_ref, in_refs, groups):
    me = lax.axis_index("ctx")
    for members, ref in zip(received(place_ref.shape[0], groups), in_refs):
        for i, turn in enumerate(members):
            if turn is not None:
                place_ref[me ^ turn] = ref[i]


def scatter(out_refs, place_ref, groups):
    me = lax.axis_index("ctx")
    for members, ref in zip(sent(place_ref.shape[0], groups), out_refs):
        for i, turn in enumerate(members):
            ref[i] = place_ref[me ^ turn]


def gate_kernel(first_hbm, values_hbm, grad_hbm, second_hbm, filters_hbm, gain_hbm, *refs):
    *out_refs, kept_ref, all_ref, filters_ref, gain_ref, sems = refs
    gates = [kept_ref.at[i] for i in range(4)]
    sources = (first_hbm, values_hbm, filters_hbm, gain_hbm, grad_hbm, second_hbm)
    places = (*gates[:2], filters_ref, gain_ref, *gates[2:])
    copies = [pltpu.make_async_copy(source, place, sems.at[i]) for i, (source, place) in enumerate(zip(sources, places))]
    for copy in copies:
        copy.start()
    shards = all_ref.shape[0]
    channels, blocks = filters_ref.shape
    me = lax.axis_index("ctx")

    def place(s, signal):
        for j in range(blocks // LANES):
            tile = signal[:, j * LANES : (j + 1) * LANES].reshape(shards, ROWS, LANES)
            all_ref[:, s, :, j * LANES : (j + 1) * LANES] = tile

    copies[0].wait()
    copies[1].wait()
    place(0, kept_ref[0].astype(jnp.float32) * kept_ref[1].astype(jnp.float32))
    copies[2].wait()
    copies[3].wait()
    shape = (channels, channels)
    diagonal = lax.broadcasted_iota(jnp.int32, shape, 0) == lax.broadcasted_iota(jnp.int32, shape, 1)
    gain = jnp.sum(jnp.where(diagonal, gain_ref[...], 0.0), axis=1, keepdims=True)
    position = me * blocks + lax.broadcasted_iota(jnp.int32, (channels, blocks), 1)
    place(1, filters_ref[...] + jnp.where(position == 0, gain, 0.0))
    copies[4].wait()
    copies[5].wait()
    place(2, kept_ref[2].astype(jnp.float32) * kept_ref[3].astype(jnp.float32))
    scatter(out_refs, all_ref, OUTWARD)


def spectral_kernel(outer_ref, back_ref, forward_ref, inverse_ref, twist_ref, *refs):
    *refs, all_ref, in_ref = refs
    shards = in_ref.shape[0]
    count = len(received(shards, OUTWARD))
    in_refs, out_refs = refs[:count], refs[count:]
    gather(in_ref, in_refs, OUTWARD)
    tiles = in_ref.shape[3] // LANES
    span = tiles * ROWS
    rows = shards * span
    spec_rows = rows + ROWS
    cosine, sine = twist_ref[0], twist_ref[1]

    def take(s):
        parts = [in_ref[:, s, :, j * LANES : (j + 1) * LANES] for j in range(tiles)]
        return jnp.stack(parts, axis=1).reshape(rows, LANES)

    signals = [take(s) for s in range(3)]
    total = jnp.sum((signals[0] * signals[2]).reshape(rows // ROWS, ROWS, LANES), axis=0)
    total = jnp.broadcast_to(jnp.sum(total, axis=1, keepdims=True), (ROWS, LANES))
    all_ref[:, 3 * span :, :] = jnp.broadcast_to(total[None], (shards, ROWS, LANES))
    columns = long_dot(outer_ref, split(jnp.concatenate(signals, axis=1)))
    edge = jnp.zeros((ROWS, LANES), jnp.float32)
    spectra = []
    for s in range(3):
        lanes = slice(s * LANES, (s + 1) * LANES)
        real = columns[:spec_rows, lanes]
        imag = jnp.concatenate([edge, columns[spec_rows:, lanes], edge], axis=0)
        turned = jnp.concatenate([real * cosine - imag * sine, -(real * sine + imag * cosine)], axis=1)
        spectra.append(long_dot(split(turned), forward_ref))
    (mr, mi), (fr, fi), (cr, ci) = [(x[:, :LANES], x[:, LANES:]) for x in spectra]
    products = (
        (fr * mr - fi * mi, fr * mi + fi * mr),
        (fr * cr + fi * ci, fr * ci - fi * cr),
        (mr * cr + mi * ci, mr * ci - mi * cr),
    )
    reverted = []
    for real, imag in products:
        waves = long_dot(split(jnp.concatenate([real, imag], axis=1)), inverse_ref)
        real, imag = waves[:, :LANES], waves[:, LANES:]
        turned_imag = real * sine + imag * cosine
        reverted.append(jnp.concatenate([real * cosine - imag * sine, turned_imag[ROWS:-ROWS]], axis=0))
    result = long_dot(back_ref, split(jnp.concatenate(reverted, axis=1)))
    for s in range(3):
        all_ref[:, s * span : (s + 1) * span, :] = result[:, s * LANES : (s + 1) * LANES].reshape(shards, span, LANES)
    scatter(out_refs, all_ref, HOMEWARD)


def output_kernel(kept_ref, *refs):
    _, channels, blocks = kept_ref.shape
    tiles = blocks // LANES
    count = len(received(channels // ROWS, HOMEWARD))
    in_refs, (out_ref, gfirst_ref, gsecond_ref, gvalues_ref, gfilters_ref, gskip_ref, result_ref, total_ref) = refs[:count], refs[count:]
    me = lax.axis_index("ctx")
    for members, ref in zip(received(channels // ROWS, HOMEWARD), in_refs):
        for i, turn in enumerate(members):
            if turn is None:
                continue
            own = pl.ds(pl.multiple_of((me ^ turn) * ROWS, ROWS), ROWS)
            for s, dst_ref in enumerate((result_ref.at[0], result_ref.at[1], gfilters_ref)):
                for j in range(tiles):
                    dst_ref[own, j * LANES : (j + 1) * LANES] = ref[i, (s * tiles + j) * ROWS : (s * tiles + j + 1) * ROWS, :]
            total_ref[own, :] = ref[i, 3 * tiles * ROWS :, :]
    first, values, grad, second = [kept_ref[i].astype(jnp.float32) for i in range(4)]
    before = result_ref[0]
    out_ref[...] = second * before
    gsecond_ref[...] = grad * before
    back = result_ref[1]
    gfirst_ref[...] = back * values
    gvalues_ref[...] = back * first
    shape = (channels, channels)
    diagonal = lax.broadcasted_iota(jnp.int32, shape, 0) == lax.broadcasted_iota(jnp.int32, shape, 1)
    gskip_ref[...] = jnp.sum(jnp.where(diagonal, total_ref[:, :channels], 0.0), axis=0, keepdims=True)


def call(kernel, out_shape, args, scratch_shapes=()):
    return pl.pallas_call(
        kernel,
        out_shape=out_shape,
        in_specs=[VMEM] * len(args),
        out_specs=[VMEM] * len(out_shape),
        scratch_shapes=scratch_shapes,
        compiler_params=PARAMS,
    )(*args)


def by_channels(first_gate, second_gate, values, filters, skip_gain, grad_output):
    channels, blocks = filters.shape
    shards = lax.axis_size("ctx")
    tiles = blocks // LANES
    length = blocks * shards
    rows = length // LANES * ROWS
    wide, half = jnp.float32, jnp.bfloat16
    sources = (first_gate, values, grad_output, second_gate, filters, skip_gain.reshape(1, channels))
    slab = (3, ROWS, blocks)
    outs = [pltpu.VMEM((len(members), *slab), wide) for members in sent(shards, OUTWARD)]
    *slabs, kept = pl.pallas_call(
        gate_kernel,
        out_shape=[*outs, pltpu.VMEM((4, channels, blocks), half)],
        in_specs=[HBM] * len(sources),
        out_specs=[VMEM] * (len(outs) + 1),
        scratch_shapes=[
            pltpu.VMEM((shards, *slab), wide),
            pltpu.VMEM((channels, blocks), wide),
            pltpu.VMEM((1, channels), wide),
            pltpu.SemaphoreType.DMA((len(sources),)),
        ],
        compiler_params=PARAMS,
    )(*[pltpu.with_memory_space_constraint(source, pltpu.HBM) for source in sources])
    tables = call(
        table_kernel,
        [
            pltpu.VMEM((2, 2 * rows, rows), half),
            pltpu.VMEM((2, rows, 2 * rows), half),
            pltpu.VMEM((2, 2 * LANES, 2 * LANES), half),
            pltpu.VMEM((2, 2 * LANES, 2 * LANES), half),
            pltpu.VMEM((2, rows + ROWS, LANES), wide),
        ],
        [jnp.asarray(make_tables(length))],
    )
    result = ((3 * tiles + 1) * ROWS, LANES)
    slabs = call(
        spectral_kernel,
        [pltpu.VMEM((len(members), *result), wide) for members in sent(shards, HOMEWARD)],
        (*tables, *swap(slabs, OUTWARD)),
        [pltpu.VMEM((shards, *result), wide), pltpu.VMEM((shards, *slab), wide)],
    )
    *full, grad_skip = call(
        output_kernel,
        [jax.ShapeDtypeStruct((channels, blocks), wide)] * 5 + [jax.ShapeDtypeStruct((1, channels), wide)],
        (kept, *swap(slabs, HOMEWARD)),
        [pltpu.VMEM((2, channels, blocks), wide), pltpu.VMEM((channels, LANES), wide)],
    )
    return (*full, grad_skip.reshape(channels))


def turn_table(first_index, second_index, period):
    product = first_index[:, None] * second_index[None, :] % period
    angles = 2.0 * math.pi / period * product.astype(jnp.float32)
    return (jnp.cos(angles), jnp.sin(angles))


def right_dot(data, table):
    return jnp.dot(data, table, precision=HIGHEST)


def by_columns(first_gate, second_gate, values, filters, skip_gain, grad_output):
    channels, length = filters.shape
    shards = lax.axis_size("ctx")
    blocks = length // shards
    position = lax.axis_index("ctx")
    period = 2 * shards * length
    first = first_gate.astype(jnp.float32)
    second = second_gate.astype(jnp.float32)
    values_wide = values.astype(jnp.float32)
    mixed = first * values_wide
    carried = grad_output.astype(jnp.float32) * second
    signal = jnp.stack([mixed, filters, carried]).reshape(3, channels, blocks, shards)
    spread = lax.all_to_all(signal, "ctx", split_axis=3, concat_axis=3, tiled=True)
    shard_index = jnp.arange(shards, dtype=jnp.int32)
    cosine, sines = turn_table(shard_index, shard_index, 2 * shards)
    parity = (1 - 2 * (shard_index % 2)).astype(jnp.float32)
    fwd_real = jnp.stack([cosine, parity[:, None] * cosine], axis=1)
    fwd_imag = jnp.stack([-sines, -parity[:, None] * sines], axis=1)
    real_part = jnp.einsum("scbm,mjk->scjbk", spread, fwd_real, precision=HIGHEST)
    imag_part = jnp.einsum("scbm,mjk->scjbk", spread, fwd_imag, precision=HIGHEST)
    sectioned = jnp.stack([real_part, imag_part])
    moved = lax.all_to_all(sectioned, "ctx", split_axis=5, concat_axis=5, tiled=True).reshape(
        2, 3, channels, 2, length
    )
    col_real = moved[0]
    col_imag = moved[1]
    col_index = jnp.stack([position, position + shards])
    line_index = jnp.arange(length, dtype=jnp.int32)
    twist_cos, twist_sin = turn_table(col_index, line_index, period)
    turned_real = col_real * twist_cos + col_imag * twist_sin
    turned_imag = col_imag * twist_cos - col_real * twist_sin
    wave_cos, wave_sin = turn_table(line_index, line_index, length)
    spec_real = right_dot(turned_real, wave_cos) + right_dot(turned_imag, wave_sin)
    spec_imag = right_dot(turned_imag, wave_cos) - right_dot(turned_real, wave_sin)
    mixed_real, filter_real, carry_real = (spec_real[0], spec_real[1], spec_real[2])
    mixed_imag, filter_imag, carry_imag = (spec_imag[0], spec_imag[1], spec_imag[2])
    prod_real = jnp.stack(
        [
            filter_real * mixed_real - filter_imag * mixed_imag,
            filter_real * carry_real + filter_imag * carry_imag,
            mixed_real * carry_real + mixed_imag * carry_imag,
        ]
    )
    prod_imag = jnp.stack(
        [
            filter_real * mixed_imag + filter_imag * mixed_real,
            filter_real * carry_imag - filter_imag * carry_real,
            mixed_real * carry_imag - mixed_imag * carry_real,
        ]
    )
    back_real = right_dot(prod_real, wave_cos) - right_dot(prod_imag, wave_sin)
    back_imag = right_dot(prod_real, wave_sin) + right_dot(prod_imag, wave_cos)
    reverted_real = back_real * twist_cos - back_imag * twist_sin
    reverted_imag = back_real * twist_sin + back_imag * twist_cos
    packed = jnp.stack([reverted_real, reverted_imag])
    returned = lax.all_to_all(
        packed.reshape(2, 3, channels, 2, blocks, shards),
        "ctx",
        split_axis=5,
        concat_axis=5,
        tiled=True,
    )
    inv_real = jnp.stack([cosine, cosine * parity[None, :]])
    inv_imag = jnp.stack([-sines, -sines * parity[None, :]])
    timed = jnp.einsum("scjbk,jkm->scbm", returned[0], inv_real, precision=HIGHEST)
    timed = timed + jnp.einsum("scjbk,jkm->scbm", returned[1], inv_imag, precision=HIGHEST)
    timed = timed * (1.0 / period)
    result = lax.all_to_all(timed, "ctx", split_axis=3, concat_axis=3, tiled=True).reshape(
        3, channels, length
    )
    gain = skip_gain[:, None]
    before = result[0] + gain * mixed
    output = second * before
    grad_second = grad_output.astype(jnp.float32) * before
    back_mixed = result[1] + gain * carried
    grad_first = back_mixed * values_wide
    grad_values = back_mixed * first
    grad_filters = result[2]
    grad_skip = lax.psum(jnp.sum(carried * mixed, axis=1), "ctx")
    return (output, grad_first, grad_second, grad_values, grad_filters, grad_skip)


def per_device(first_gate, second_gate, values, filters, skip_gain, grad_output):
    channels, blocks = filters.shape
    shards = lax.axis_size("ctx")
    fits = channels == ROWS * shards and shards & (shards - 1) == 0 and blocks % LANES == 0 and channels <= LANES
    plan = by_channels if fits else by_columns
    return plan(first_gate, second_gate, values, filters, skip_gain, grad_output)


def solution(mesh):
    placed = (
        P("chan", ("groups", "ctx")),
        P("chan", ("groups", "ctx")),
        P("chan", ("groups", "ctx")),
        P("chan", ("groups", "ctx")),
        P("chan"),
        P("chan", ("groups", "ctx")),
    )
    return jax.shard_map(
        per_device,
        mesh=mesh,
        in_specs=placed,
        out_specs=(
            P("chan", ("groups", "ctx")),
            P("chan", ("groups", "ctx")),
            P("chan", ("groups", "ctx")),
            P("chan", ("groups", "ctx")),
            P("chan", ("groups", "ctx")),
            P(("groups", "chan")),
        ),
        check_vma=False,
    )
```

```python
import math

import jax
import jax.numpy as jnp
import numpy as np
from jax import lax
from jax.experimental import pallas as pl
from jax.experimental.pallas import tpu as pltpu
from jax.sharding import PartitionSpec as P

HIGHEST = lax.Precision.HIGHEST
OUTWARD = ((6, 7), (1, 3), (2,), (5,), (4,))
HOMEWARD = ((6, 7), (1, 3), (4,), (2,), (5,))
LANES = 128
ROWS = 8
VMEM = pl.BlockSpec(memory_space=pltpu.VMEM)
HBM = pl.BlockSpec(memory_space=pltpu.HBM)
PARAMS = pltpu.CompilerParams(vmem_limit_bytes=48 * 1024 * 1024)


def make_tables(length):
    groups = length // LANES
    period = 2 * length
    turns = 2 * groups
    k1 = np.arange(groups + 1)
    inner = k1[1:-1]
    a = np.arange(groups)
    b = np.arange(LANES)
    cosine = np.cos(2.0 * np.pi / turns * (k1[:, None] * a % turns))
    sine = np.sin(2.0 * np.pi / turns * (inner[:, None] * a % turns))
    weight = np.where((k1 == 0) | (k1 == groups), 1.0, 2.0) / period
    outer = np.concatenate([cosine, sine])
    back = np.concatenate([weight[:, None] * cosine, -2.0 / period * sine]).T
    wave = 2.0 * np.pi / LANES * (b[:, None] * b % LANES)
    twist = 2.0 * np.pi / period * (k1[:, None] * b % period)
    parts = [np.repeat(outer, ROWS, axis=1), np.repeat(back, ROWS, axis=1)]
    parts = [np.concatenate(np.split(part, part.shape[1] // LANES, axis=1)) for part in parts]
    parts += [np.cos(wave), np.sin(wave), np.cos(twist), np.sin(twist)]
    parts.append(np.zeros((-2 * (groups + 1) % ROWS, LANES)))
    return np.concatenate(parts).astype(np.float32)


def spread_rows(table, masked):
    rows, columns = table.shape
    wide = jnp.broadcast_to(table[:, None, :], (rows, ROWS, columns))
    if masked:
        shape = (ROWS, columns)
        own = lax.broadcasted_iota(jnp.int32, shape, 0) == lax.broadcasted_iota(jnp.int32, shape, 1) % ROWS
        wide = jnp.where(own[None], wide, 0.0)
    return wide.reshape(rows * ROWS, columns)


def split(data):
    high = data.astype(jnp.bfloat16)
    return high, (data - high.astype(jnp.float32)).astype(jnp.bfloat16)


def dot(left, right):
    return jnp.dot(left, right, preferred_element_type=jnp.float32)


def long_dot(left, right):
    return dot(left[0], right[0]) + (dot(left[0], right[1]) + dot(left[1], right[0]))


def table_kernel(in_ref, outer_ref, back_ref, forward_ref, inverse_ref, twist_ref):
    groups = outer_ref.shape[2] // ROWS
    tiles = outer_ref.shape[2] // LANES
    row = 0

    def take(rows, pieces=1):
        nonlocal row
        parts = [in_ref[row + i * rows : row + (i + 1) * rows, :] for i in range(pieces)]
        row += rows * pieces
        return jnp.concatenate(parts, axis=1)

    outer_ref[0], outer_ref[1] = split(spread_rows(take(2 * groups, tiles), True))
    back_ref[0], back_ref[1] = split(spread_rows(take(groups, 2 * tiles), True))
    cosine, sine = split(take(LANES)), split(take(LANES))
    for i, (c, s) in enumerate(zip(cosine, sine)):
        forward_ref[i] = jnp.concatenate([jnp.concatenate([c, -s], axis=1), jnp.concatenate([s, c], axis=1)], axis=0)
        inverse_ref[i] = jnp.concatenate([jnp.concatenate([c, s], axis=1), jnp.concatenate([-s, c], axis=1)], axis=0)
    twist_ref[0] = spread_rows(take(groups + 1), False)
    twist_ref[1] = spread_rows(take(groups + 1), False)


def sent(shards, groups):
    if sum(map(len, groups)) != shards - 1:
        groups = tuple((turn,) for turn in range(shards - 1, 0, -1))
    return (*groups, (0,))


def received(shards, groups):
    groups = sent(shards, groups)
    first = [(group[0], *(None for _ in group[1:])) for group in groups]
    return (*first[:-1], *((turn,) for group in groups for turn in group[1:]), (0,))


def swap(arrays, groups):
    *arrays, own = arrays
    shards = lax.axis_size("ctx")

    def move(array, turn):
        return lax.ppermute(array, "ctx", [(i, i ^ turn) for i in range(shards)])

    moved, relayed = [], []
    for members, array in zip(sent(shards, groups), arrays):
        moved.append(move(array, members[0]))
        relayed += [move(moved[-1][i : i + 1], members[0] ^ members[i]) for i in range(1, len(members))]
    return (*moved, *relayed, own)


def gather(place_ref, in_refs, groups):
    me = lax.axis_index("ctx")
    for members, ref in zip(received(place_ref.shape[0], groups), in_refs):
        for i, turn in enumerate(members):
            if turn is not None:
                place_ref[me ^ turn] = ref[i]


def scatter(out_refs, place_ref, groups):
    me = lax.axis_index("ctx")
    for members, ref in zip(sent(place_ref.shape[0], groups), out_refs):
        for i, turn in enumerate(members):
            ref[i] = place_ref[me ^ turn]


def gate_kernel(first_hbm, values_hbm, grad_hbm, second_hbm, filters_hbm, gain_hbm, *refs):
    *out_refs, kept_ref, all_ref, filters_ref, gain_ref, sems = refs
    gates = [kept_ref.at[i] for i in range(4)]
    sources = (first_hbm, values_hbm, filters_hbm, gain_hbm, grad_hbm, second_hbm)
    places = (*gates[:2], filters_ref, gain_ref, *gates[2:])
    copies = [pltpu.make_async_copy(source, place, sems.at[i]) for i, (source, place) in enumerate(zip(sources, places))]
    for copy in copies:
        copy.start()
    shards = all_ref.shape[0]
    channels, blocks = filters_ref.shape
    me = lax.axis_index("ctx")

    def place(s, signal):
        for j in range(blocks // LANES):
            tile = signal[:, j * LANES : (j + 1) * LANES].reshape(shards, ROWS, LANES)
            all_ref[:, s, :, j * LANES : (j + 1) * LANES] = tile

    copies[0].wait()
    copies[1].wait()
    place(0, kept_ref[0].astype(jnp.float32) * kept_ref[1].astype(jnp.float32))
    copies[2].wait()
    copies[3].wait()
    shape = (channels, channels)
    diagonal = lax.broadcasted_iota(jnp.int32, shape, 0) == lax.broadcasted_iota(jnp.int32, shape, 1)
    gain = jnp.sum(jnp.where(diagonal, gain_ref[...], 0.0), axis=1, keepdims=True)
    position = me * blocks + lax.broadcasted_iota(jnp.int32, (channels, blocks), 1)
    place(1, filters_ref[...] + jnp.where(position == 0, gain, 0.0))
    copies[4].wait()
    copies[5].wait()
    place(2, kept_ref[2].astype(jnp.float32) * kept_ref[3].astype(jnp.float32))
    scatter(out_refs, all_ref, OUTWARD)


def spectral_kernel(outer_ref, back_ref, forward_ref, inverse_ref, twist_ref, *refs):
    *refs, all_ref, in_ref = refs
    shards = in_ref.shape[0]
    count = len(received(shards, OUTWARD))
    in_refs, out_refs = refs[:count], refs[count:]
    gather(in_ref, in_refs, OUTWARD)
    tiles = in_ref.shape[3] // LANES
    span = tiles * ROWS
    rows = shards * span
    spec_rows = rows + ROWS
    cosine, sine = twist_ref[0], twist_ref[1]

    def take(s):
        parts = [in_ref[:, s, :, j * LANES : (j + 1) * LANES] for j in range(tiles)]
        return jnp.stack(parts, axis=1).reshape(rows, LANES)

    signals = [take(s) for s in range(3)]
    total = jnp.sum((signals[0] * signals[2]).reshape(rows // ROWS, ROWS, LANES), axis=0)
    total = jnp.broadcast_to(jnp.sum(total, axis=1, keepdims=True), (ROWS, LANES))
    all_ref[:, 3 * span :, :] = jnp.broadcast_to(total[None], (shards, ROWS, LANES))
    columns = long_dot(outer_ref, split(jnp.concatenate(signals, axis=1)))
    edge = jnp.zeros((ROWS, LANES), jnp.float32)
    spectra = []
    for s in range(3):
        lanes = slice(s * LANES, (s + 1) * LANES)
        real = columns[:spec_rows, lanes]
        imag = jnp.concatenate([edge, columns[spec_rows:, lanes], edge], axis=0)
        turned = jnp.concatenate([real * cosine - imag * sine, -(real * sine + imag * cosine)], axis=1)
        spectra.append(long_dot(split(turned), forward_ref))
    (mr, mi), (fr, fi), (cr, ci) = [(x[:, :LANES], x[:, LANES:]) for x in spectra]
    products = (
        (fr * mr - fi * mi, fr * mi + fi * mr),
        (fr * cr + fi * ci, fr * ci - fi * cr),
        (mr * cr + mi * ci, mr * ci - mi * cr),
    )
    reverted = []
    for real, imag in products:
        waves = long_dot(split(jnp.concatenate([real, imag], axis=1)), inverse_ref)
        real, imag = waves[:, :LANES], waves[:, LANES:]
        turned_imag = real * sine + imag * cosine
        reverted.append(jnp.concatenate([real * cosine - imag * sine, turned_imag[ROWS:-ROWS]], axis=0))
    result = long_dot(back_ref, split(jnp.concatenate(reverted, axis=1)))
    for s in range(3):
        all_ref[:, s * span : (s + 1) * span, :] = result[:, s * LANES : (s + 1) * LANES].reshape(shards, span, LANES)
    scatter(out_refs, all_ref, HOMEWARD)


def output_kernel(kept_ref, *refs):
    _, channels, blocks = kept_ref.shape
    tiles = blocks // LANES
    count = len(received(channels // ROWS, HOMEWARD))
    in_refs, (out_ref, gfirst_ref, gsecond_ref, gvalues_ref, gfilters_ref, gskip_ref, result_ref, total_ref) = refs[:count], refs[count:]
    me = lax.axis_index("ctx")
    for members, ref in zip(received(channels // ROWS, HOMEWARD), in_refs):
        for i, turn in enumerate(members):
            if turn is None:
                continue
            own = pl.ds(pl.multiple_of((me ^ turn) * ROWS, ROWS), ROWS)
            for s, dst_ref in enumerate((result_ref.at[0], result_ref.at[1], gfilters_ref)):
                for j in range(tiles):
                    dst_ref[own, j * LANES : (j + 1) * LANES] = ref[i, (s * tiles + j) * ROWS : (s * tiles + j + 1) * ROWS, :]
            total_ref[own, :] = ref[i, 3 * tiles * ROWS :, :]
    first, values, grad, second = [kept_ref[i].astype(jnp.float32) for i in range(4)]
    before = result_ref[0]
    out_ref[...] = second * before
    gsecond_ref[...] = grad * before
    back = result_ref[1]
    gfirst_ref[...] = back * values
    gvalues_ref[...] = back * first
    shape = (channels, channels)
    diagonal = lax.broadcasted_iota(jnp.int32, shape, 0) == lax.broadcasted_iota(jnp.int32, shape, 1)
    gskip_ref[...] = jnp.sum(jnp.where(diagonal, total_ref[:, :channels], 0.0), axis=0, keepdims=True)


def call(kernel, out_shape, args, scratch_shapes=()):
    return pl.pallas_call(
        kernel,
        out_shape=out_shape,
        in_specs=[VMEM] * len(args),
        out_specs=[VMEM] * len(out_shape),
        scratch_shapes=scratch_shapes,
        compiler_params=PARAMS,
    )(*args)


def by_channels(first_gate, second_gate, values, filters, skip_gain, grad_output):
    channels, blocks = filters.shape
    shards = lax.axis_size("ctx")
    tiles = blocks // LANES
    length = blocks * shards
    rows = length // LANES * ROWS
    wide, half = jnp.float32, jnp.bfloat16
    sources = (first_gate, values, grad_output, second_gate, filters, skip_gain.reshape(1, channels))
    slab = (3, ROWS, blocks)
    outs = [pltpu.VMEM((len(members), *slab), wide) for members in sent(shards, OUTWARD)]
    *slabs, kept = pl.pallas_call(
        gate_kernel,
        out_shape=[*outs, pltpu.VMEM((4, channels, blocks), half)],
        in_specs=[HBM] * len(sources),
        out_specs=[VMEM] * (len(outs) + 1),
        scratch_shapes=[
            pltpu.VMEM((shards, *slab), wide),
            pltpu.VMEM((channels, blocks), wide),
            pltpu.VMEM((1, channels), wide),
            pltpu.SemaphoreType.DMA((len(sources),)),
        ],
        compiler_params=PARAMS,
    )(*[pltpu.with_memory_space_constraint(source, pltpu.HBM) for source in sources])
    tables = call(
        table_kernel,
        [
            pltpu.VMEM((2, 2 * rows, rows), half),
            pltpu.VMEM((2, rows, 2 * rows), half),
            pltpu.VMEM((2, 2 * LANES, 2 * LANES), half),
            pltpu.VMEM((2, 2 * LANES, 2 * LANES), half),
            pltpu.VMEM((2, rows + ROWS, LANES), wide),
        ],
        [jnp.asarray(make_tables(length))],
    )
    result = ((3 * tiles + 1) * ROWS, LANES)
    slabs = call(
        spectral_kernel,
        [pltpu.VMEM((len(members), *result), wide) for members in sent(shards, HOMEWARD)],
        (*tables, *swap(slabs, OUTWARD)),
        [pltpu.VMEM((shards, *result), wide), pltpu.VMEM((shards, *slab), wide)],
    )
    *full, grad_skip = call(
        output_kernel,
        [jax.ShapeDtypeStruct((channels, blocks), wide)] * 5 + [jax.ShapeDtypeStruct((1, channels), wide)],
        (kept, *swap(slabs, HOMEWARD)),
        [pltpu.VMEM((2, channels, blocks), wide), pltpu.VMEM((channels, LANES), wide)],
    )
    return (*full, grad_skip.reshape(channels))


def turn_table(first_index, second_index, period):
    product = first_index[:, None] * second_index[None, :] % period
    angles = 2.0 * math.pi / period * product.astype(jnp.float32)
    return (jnp.cos(angles), jnp.sin(angles))


def right_dot(data, table):
    return jnp.dot(data, table, precision=HIGHEST)


def by_columns(first_gate, second_gate, values, filters, skip_gain, grad_output):
    channels, length = filters.shape
    shards = lax.axis_size("ctx")
    blocks = length // shards
    position = lax.axis_index("ctx")
    period = 2 * shards * length
    first = first_gate.astype(jnp.float32)
    second = second_gate.astype(jnp.float32)
    values_wide = values.astype(jnp.float32)
    mixed = first * values_wide
    carried = grad_output.astype(jnp.float32) * second
    signal = jnp.stack([mixed, filters, carried]).reshape(3, channels, blocks, shards)
    spread = lax.all_to_all(signal, "ctx", split_axis=3, concat_axis=3, tiled=True)
    shard_index = jnp.arange(shards, dtype=jnp.int32)
    cosine, sines = turn_table(shard_index, shard_index, 2 * shards)
    parity = (1 - 2 * (shard_index % 2)).astype(jnp.float32)
    fwd_real = jnp.stack([cosine, parity[:, None] * cosine], axis=1)
    fwd_imag = jnp.stack([-sines, -parity[:, None] * sines], axis=1)
    real_part = jnp.einsum("scbm,mjk->scjbk", spread, fwd_real, precision=HIGHEST)
    imag_part = jnp.einsum("scbm,mjk->scjbk", spread, fwd_imag, precision=HIGHEST)
    sectioned = jnp.stack([real_part, imag_part])
    moved = lax.all_to_all(sectioned, "ctx", split_axis=5, concat_axis=5, tiled=True).reshape(
        2, 3, channels, 2, length
    )
    col_real = moved[0]
    col_imag = moved[1]
    col_index = jnp.stack([position, position + shards])
    line_index = jnp.arange(length, dtype=jnp.int32)
    twist_cos, twist_sin = turn_table(col_index, line_index, period)
    turned_real = col_real * twist_cos + col_imag * twist_sin
    turned_imag = col_imag * twist_cos - col_real * twist_sin
    wave_cos, wave_sin = turn_table(line_index, line_index, length)
    spec_real = right_dot(turned_real, wave_cos) + right_dot(turned_imag, wave_sin)
    spec_imag = right_dot(turned_imag, wave_cos) - right_dot(turned_real, wave_sin)
    mixed_real, filter_real, carry_real = (spec_real[0], spec_real[1], spec_real[2])
    mixed_imag, filter_imag, carry_imag = (spec_imag[0], spec_imag[1], spec_imag[2])
    prod_real = jnp.stack(
        [
            filter_real * mixed_real - filter_imag * mixed_imag,
            filter_real * carry_real + filter_imag * carry_imag,
            mixed_real * carry_real + mixed_imag * carry_imag,
        ]
    )
    prod_imag = jnp.stack(
        [
            filter_real * mixed_imag + filter_imag * mixed_real,
            filter_real * carry_imag - filter_imag * carry_real,
            mixed_real * carry_imag - mixed_imag * carry_real,
        ]
    )
    back_real = right_dot(prod_real, wave_cos) - right_dot(prod_imag, wave_sin)
    back_imag = right_dot(prod_real, wave_sin) + right_dot(prod_imag, wave_cos)
    reverted_real = back_real * twist_cos - back_imag * twist_sin
    reverted_imag = back_real * twist_sin + back_imag * twist_cos
    packed = jnp.stack([reverted_real, reverted_imag])
    returned = lax.all_to_all(
        packed.reshape(2, 3, channels, 2, blocks, shards),
        "ctx",
        split_axis=5,
        concat_axis=5,
        tiled=True,
    )
    inv_real = jnp.stack([cosine, cosine * parity[None, :]])
    inv_imag = jnp.stack([-sines, -sines * parity[None, :]])
    timed = jnp.einsum("scjbk,jkm->scbm", returned[0], inv_real, precision=HIGHEST)
    timed = timed + jnp.einsum("scjbk,jkm->scbm", returned[1], inv_imag, precision=HIGHEST)
    timed = timed * (1.0 / period)
    result = lax.all_to_all(timed, "ctx", split_axis=3, concat_axis=3, tiled=True).reshape(
        3, channels, length
    )
    gain = skip_gain[:, None]
    before = result[0] + gain * mixed
    output = second * before
    grad_second = grad_output.astype(jnp.float32) * before
    back_mixed = result[1] + gain * carried
    grad_first = back_mixed * values_wide
    grad_values = back_mixed * first
    grad_filters = result[2]
    grad_skip = lax.psum(jnp.sum(carried * mixed, axis=1), "ctx")
    return (output, grad_first, grad_second, grad_values, grad_filters, grad_skip)


def per_device(first_gate, second_gate, values, filters, skip_gain, grad_output):
    channels, blocks = filters.shape
    shards = lax.axis_size("ctx")
    fits = channels == ROWS * shards and shards & (shards - 1) == 0 and blocks % LANES == 0 and channels <= LANES
    plan = by_channels if fits else by_columns
    return plan(first_gate, second_gate, values, filters, skip_gain, grad_output)


def solution(mesh):
    placed = (
        P("chan", ("groups", "ctx")),
        P("chan", ("groups", "ctx")),
        P("chan", ("groups", "ctx")),
        P("chan", ("groups", "ctx")),
        P("chan"),
        P("chan", ("groups", "ctx")),
    )
    return jax.shard_map(
        per_device,
        mesh=mesh,
        in_specs=placed,
        out_specs=(
            P("chan", ("groups", "ctx")),
            P("chan", ("groups", "ctx")),
            P("chan", ("groups", "ctx")),
            P("chan", ("groups", "ctx")),
            P("chan", ("groups", "ctx")),
            P(("groups", "chan")),
        ),
        check_vma=False,
    )
```

```python
import math

import jax
import jax.numpy as jnp
import numpy as np
from jax import lax
from jax.experimental import pallas as pl
from jax.experimental.pallas import tpu as pltpu
from jax.sharding import PartitionSpec as P

HIGHEST = lax.Precision.HIGHEST
OUTWARD = ((6, 7), (1, 3), (2,), (5,), (4,))
HOMEWARD = ((6, 7), (1, 3), (4,), (2,), (5,))
LANES = 128
ROWS = 8
VMEM = pl.BlockSpec(memory_space=pltpu.VMEM)
HBM = pl.BlockSpec(memory_space=pltpu.HBM)
PARAMS = pltpu.CompilerParams(vmem_limit_bytes=48 * 1024 * 1024)


def make_tables(length):
    groups = length // LANES
    period = 2 * length
    turns = 2 * groups
    k1 = np.arange(groups + 1)
    inner = k1[1:-1]
    a = np.arange(groups)
    b = np.arange(LANES)
    cosine = np.cos(2.0 * np.pi / turns * (k1[:, None] * a % turns))
    sine = np.sin(2.0 * np.pi / turns * (inner[:, None] * a % turns))
    weight = np.where((k1 == 0) | (k1 == groups), 1.0, 2.0) / period
    outer = np.concatenate([cosine, sine])
    back = np.concatenate([weight[:, None] * cosine, -2.0 / period * sine]).T
    wave = 2.0 * np.pi / LANES * (b[:, None] * b % LANES)
    twist = 2.0 * np.pi / period * (k1[:, None] * b % period)
    parts = [np.repeat(outer, ROWS, axis=1), np.repeat(back, ROWS, axis=1)]
    parts = [np.concatenate(np.split(part, part.shape[1] // LANES, axis=1)) for part in parts]
    parts += [np.cos(wave), np.sin(wave), np.cos(twist), np.sin(twist)]
    parts.append(np.zeros((-2 * (groups + 1) % ROWS, LANES)))
    return np.concatenate(parts).astype(np.float32)


def spread_rows(table, masked):
    rows, columns = table.shape
    wide = jnp.broadcast_to(table[:, None, :], (rows, ROWS, columns))
    if masked:
        shape = (ROWS, columns)
        own = lax.broadcasted_iota(jnp.int32, shape, 0) == lax.broadcasted_iota(jnp.int32, shape, 1) % ROWS
        wide = jnp.where(own[None], wide, 0.0)
    return wide.reshape(rows * ROWS, columns)


def split(data):
    high = data.astype(jnp.bfloat16)
    return high, (data - high.astype(jnp.float32)).astype(jnp.bfloat16)


def dot(left, right):
    return jnp.dot(left, right, preferred_element_type=jnp.float32)


def long_dot(left, right):
    return dot(left[0], right[0]) + (dot(left[0], right[1]) + dot(left[1], right[0]))


def table_dot(table, data):
    high, low = split(data)
    both = dot(table[0], jnp.concatenate([high, low], axis=1))
    columns = data.shape[1]
    return both[:, :columns] + (both[:, columns:] + dot(table[1], high))


def table_kernel(in_ref, outer_ref, back_ref, forward_ref, inverse_ref, twist_ref):
    groups = outer_ref.shape[2] // ROWS
    tiles = outer_ref.shape[2] // LANES
    row = 0

    def take(rows, pieces=1):
        nonlocal row
        parts = [in_ref[row + i * rows : row + (i + 1) * rows, :] for i in range(pieces)]
        row += rows * pieces
        return jnp.concatenate(parts, axis=1)

    outer_ref[0], outer_ref[1] = split(spread_rows(take(2 * groups, tiles), True))
    back_ref[0], back_ref[1] = split(spread_rows(take(groups, 2 * tiles), True))
    cosine, sine = split(take(LANES)), split(take(LANES))
    for i, (c, s) in enumerate(zip(cosine, sine)):
        forward_ref[i] = jnp.concatenate([jnp.concatenate([c, -s], axis=1), jnp.concatenate([s, c], axis=1)], axis=0)
        inverse_ref[i] = jnp.concatenate([jnp.concatenate([c, s], axis=1), jnp.concatenate([-s, c], axis=1)], axis=0)
    twist_ref[0] = spread_rows(take(groups + 1), False)
    twist_ref[1] = spread_rows(take(groups + 1), False)


def sent(shards, groups):
    if sum(map(len, groups)) != shards - 1:
        groups = tuple((turn,) for turn in range(shards - 1, 0, -1))
    return (*groups, (0,))


def received(shards, groups):
    groups = sent(shards, groups)
    first = [(group[0], *(None for _ in group[1:])) for group in groups]
    return (*first[:-1], *((turn,) for group in groups for turn in group[1:]), (0,))


def swap(arrays, groups):
    *arrays, own = arrays
    shards = lax.axis_size("ctx")

    def move(array, turn):
        return lax.ppermute(array, "ctx", [(i, i ^ turn) for i in range(shards)])

    moved, relayed = [], []
    for members, array in zip(sent(shards, groups), arrays):
        moved.append(move(array, members[0]))
        relayed += [move(moved[-1][i : i + 1], members[0] ^ members[i]) for i in range(1, len(members))]
    return (*moved, *relayed, own)


def gather(place_ref, in_refs, groups):
    me = lax.axis_index("ctx")
    for members, ref in zip(received(place_ref.shape[0], groups), in_refs):
        for i, turn in enumerate(members):
            if turn is not None:
                place_ref[me ^ turn] = ref[i]


def scatter(out_refs, place_ref, groups):
    me = lax.axis_index("ctx")
    for members, ref in zip(sent(place_ref.shape[0], groups), out_refs):
        for i, turn in enumerate(members):
            ref[i] = place_ref[me ^ turn]


def gate_kernel(first_hbm, values_hbm, grad_hbm, second_hbm, filters_hbm, gain_hbm, *refs):
    *out_refs, kept_ref, all_ref, filters_ref, gain_ref, sems = refs
    gates = [kept_ref.at[i] for i in range(4)]
    sources = (first_hbm, values_hbm, filters_hbm, gain_hbm, grad_hbm, second_hbm)
    places = (*gates[:2], filters_ref, gain_ref, *gates[2:])
    copies = [pltpu.make_async_copy(source, place, sems.at[i]) for i, (source, place) in enumerate(zip(sources, places))]
    for copy in copies:
        copy.start()
    shards = all_ref.shape[0]
    channels, blocks = filters_ref.shape
    me = lax.axis_index("ctx")

    def place(s, signal):
        for j in range(blocks // LANES):
            tile = signal[:, j * LANES : (j + 1) * LANES].reshape(shards, ROWS, LANES)
            all_ref[:, s, :, j * LANES : (j + 1) * LANES] = tile

    copies[0].wait()
    copies[1].wait()
    place(0, kept_ref[0].astype(jnp.float32) * kept_ref[1].astype(jnp.float32))
    copies[2].wait()
    copies[3].wait()
    shape = (channels, channels)
    diagonal = lax.broadcasted_iota(jnp.int32, shape, 0) == lax.broadcasted_iota(jnp.int32, shape, 1)
    gain = jnp.sum(jnp.where(diagonal, gain_ref[...], 0.0), axis=1, keepdims=True)
    position = me * blocks + lax.broadcasted_iota(jnp.int32, (channels, blocks), 1)
    place(1, filters_ref[...] + jnp.where(position == 0, gain, 0.0))
    copies[4].wait()
    copies[5].wait()
    place(2, kept_ref[2].astype(jnp.float32) * kept_ref[3].astype(jnp.float32))
    scatter(out_refs, all_ref, OUTWARD)


def spectral_kernel(outer_ref, back_ref, forward_ref, inverse_ref, twist_ref, *refs):
    *refs, all_ref, in_ref = refs
    shards = in_ref.shape[0]
    count = len(received(shards, OUTWARD))
    in_refs, out_refs = refs[:count], refs[count:]
    gather(in_ref, in_refs, OUTWARD)
    tiles = in_ref.shape[3] // LANES
    span = tiles * ROWS
    rows = shards * span
    spec_rows = rows + ROWS
    cosine, sine = twist_ref[0], twist_ref[1]

    def take(s):
        parts = [in_ref[:, s, :, j * LANES : (j + 1) * LANES] for j in range(tiles)]
        return jnp.stack(parts, axis=1).reshape(rows, LANES)

    signals = [take(s) for s in range(3)]
    total = jnp.sum((signals[0] * signals[2]).reshape(rows // ROWS, ROWS, LANES), axis=0)
    total = jnp.broadcast_to(jnp.sum(total, axis=1, keepdims=True), (ROWS, LANES))
    all_ref[:, 3 * span :, :] = jnp.broadcast_to(total[None], (shards, ROWS, LANES))
    columns = table_dot(outer_ref, jnp.concatenate(signals, axis=1))
    edge = jnp.zeros((ROWS, LANES), jnp.float32)
    spectra = []
    for s in range(3):
        lanes = slice(s * LANES, (s + 1) * LANES)
        real = columns[:spec_rows, lanes]
        imag = jnp.concatenate([edge, columns[spec_rows:, lanes], edge], axis=0)
        turned = jnp.concatenate([real * cosine - imag * sine, -(real * sine + imag * cosine)], axis=1)
        spectra.append(long_dot(split(turned), forward_ref))
    (mr, mi), (fr, fi), (cr, ci) = [(x[:, :LANES], x[:, LANES:]) for x in spectra]
    products = (
        (fr * mr - fi * mi, fr * mi + fi * mr),
        (fr * cr + fi * ci, fr * ci - fi * cr),
        (mr * cr + mi * ci, mr * ci - mi * cr),
    )
    reverted = []
    for real, imag in products:
        waves = long_dot(split(jnp.concatenate([real, imag], axis=1)), inverse_ref)
        real, imag = waves[:, :LANES], waves[:, LANES:]
        turned_imag = real * sine + imag * cosine
        reverted.append(jnp.concatenate([real * cosine - imag * sine, turned_imag[ROWS:-ROWS]], axis=0))
    result = table_dot(back_ref, jnp.concatenate(reverted, axis=1))
    for s in range(3):
        all_ref[:, s * span : (s + 1) * span, :] = result[:, s * LANES : (s + 1) * LANES].reshape(shards, span, LANES)
    scatter(out_refs, all_ref, HOMEWARD)


def output_kernel(kept_ref, *refs):
    _, channels, blocks = kept_ref.shape
    tiles = blocks // LANES
    count = len(received(channels // ROWS, HOMEWARD))
    in_refs, (out_ref, gfirst_ref, gsecond_ref, gvalues_ref, gfilters_ref, gskip_ref, result_ref, total_ref) = refs[:count], refs[count:]
    me = lax.axis_index("ctx")
    for members, ref in zip(received(channels // ROWS, HOMEWARD), in_refs):
        for i, turn in enumerate(members):
            if turn is None:
                continue
            own = pl.ds(pl.multiple_of((me ^ turn) * ROWS, ROWS), ROWS)
            for s, dst_ref in enumerate((result_ref.at[0], result_ref.at[1], gfilters_ref)):
                for j in range(tiles):
                    dst_ref[own, j * LANES : (j + 1) * LANES] = ref[i, (s * tiles + j) * ROWS : (s * tiles + j + 1) * ROWS, :]
            total_ref[own, :] = ref[i, 3 * tiles * ROWS :, :]
    first, values, grad, second = [kept_ref[i].astype(jnp.float32) for i in range(4)]
    before = result_ref[0]
    out_ref[...] = second * before
    gsecond_ref[...] = grad * before
    back = result_ref[1]
    gfirst_ref[...] = back * values
    gvalues_ref[...] = back * first
    shape = (channels, channels)
    diagonal = lax.broadcasted_iota(jnp.int32, shape, 0) == lax.broadcasted_iota(jnp.int32, shape, 1)
    gskip_ref[...] = jnp.sum(jnp.where(diagonal, total_ref[:, :channels], 0.0), axis=0, keepdims=True)


def call(kernel, out_shape, args, scratch_shapes=()):
    return pl.pallas_call(
        kernel,
        out_shape=out_shape,
        in_specs=[VMEM] * len(args),
        out_specs=[VMEM] * len(out_shape),
        scratch_shapes=scratch_shapes,
        compiler_params=PARAMS,
    )(*args)


def by_channels(first_gate, second_gate, values, filters, skip_gain, grad_output):
    channels, blocks = filters.shape
    shards = lax.axis_size("ctx")
    tiles = blocks // LANES
    length = blocks * shards
    rows = length // LANES * ROWS
    wide, half = jnp.float32, jnp.bfloat16
    sources = (first_gate, values, grad_output, second_gate, filters, skip_gain.reshape(1, channels))
    slab = (3, ROWS, blocks)
    outs = [pltpu.VMEM((len(members), *slab), wide) for members in sent(shards, OUTWARD)]
    *slabs, kept = pl.pallas_call(
        gate_kernel,
        out_shape=[*outs, pltpu.VMEM((4, channels, blocks), half)],
        in_specs=[HBM] * len(sources),
        out_specs=[VMEM] * (len(outs) + 1),
        scratch_shapes=[
            pltpu.VMEM((shards, *slab), wide),
            pltpu.VMEM((channels, blocks), wide),
            pltpu.VMEM((1, channels), wide),
            pltpu.SemaphoreType.DMA((len(sources),)),
        ],
        compiler_params=PARAMS,
    )(*[pltpu.with_memory_space_constraint(source, pltpu.HBM) for source in sources])
    tables = call(
        table_kernel,
        [
            pltpu.VMEM((2, 2 * rows, rows), half),
            pltpu.VMEM((2, rows, 2 * rows), half),
            pltpu.VMEM((2, 2 * LANES, 2 * LANES), half),
            pltpu.VMEM((2, 2 * LANES, 2 * LANES), half),
            pltpu.VMEM((2, rows + ROWS, LANES), wide),
        ],
        [jnp.asarray(make_tables(length))],
    )
    result = ((3 * tiles + 1) * ROWS, LANES)
    slabs = call(
        spectral_kernel,
        [pltpu.VMEM((len(members), *result), wide) for members in sent(shards, HOMEWARD)],
        (*tables, *swap(slabs, OUTWARD)),
        [pltpu.VMEM((shards, *result), wide), pltpu.VMEM((shards, *slab), wide)],
    )
    *full, grad_skip = call(
        output_kernel,
        [jax.ShapeDtypeStruct((channels, blocks), wide)] * 5 + [jax.ShapeDtypeStruct((1, channels), wide)],
        (kept, *swap(slabs, HOMEWARD)),
        [pltpu.VMEM((2, channels, blocks), wide), pltpu.VMEM((channels, LANES), wide)],
    )
    return (*full, grad_skip.reshape(channels))


def turn_table(first_index, second_index, period):
    product = first_index[:, None] * second_index[None, :] % period
    angles = 2.0 * math.pi / period * product.astype(jnp.float32)
    return (jnp.cos(angles), jnp.sin(angles))


def right_dot(data, table):
    return jnp.dot(data, table, precision=HIGHEST)


def by_columns(first_gate, second_gate, values, filters, skip_gain, grad_output):
    channels, length = filters.shape
    shards = lax.axis_size("ctx")
    blocks = length // shards
    position = lax.axis_index("ctx")
    period = 2 * shards * length
    first = first_gate.astype(jnp.float32)
    second = second_gate.astype(jnp.float32)
    values_wide = values.astype(jnp.float32)
    mixed = first * values_wide
    carried = grad_output.astype(jnp.float32) * second
    signal = jnp.stack([mixed, filters, carried]).reshape(3, channels, blocks, shards)
    spread = lax.all_to_all(signal, "ctx", split_axis=3, concat_axis=3, tiled=True)
    shard_index = jnp.arange(shards, dtype=jnp.int32)
    cosine, sines = turn_table(shard_index, shard_index, 2 * shards)
    parity = (1 - 2 * (shard_index % 2)).astype(jnp.float32)
    fwd_real = jnp.stack([cosine, parity[:, None] * cosine], axis=1)
    fwd_imag = jnp.stack([-sines, -parity[:, None] * sines], axis=1)
    real_part = jnp.einsum("scbm,mjk->scjbk", spread, fwd_real, precision=HIGHEST)
    imag_part = jnp.einsum("scbm,mjk->scjbk", spread, fwd_imag, precision=HIGHEST)
    sectioned = jnp.stack([real_part, imag_part])
    moved = lax.all_to_all(sectioned, "ctx", split_axis=5, concat_axis=5, tiled=True).reshape(
        2, 3, channels, 2, length
    )
    col_real = moved[0]
    col_imag = moved[1]
    col_index = jnp.stack([position, position + shards])
    line_index = jnp.arange(length, dtype=jnp.int32)
    twist_cos, twist_sin = turn_table(col_index, line_index, period)
    turned_real = col_real * twist_cos + col_imag * twist_sin
    turned_imag = col_imag * twist_cos - col_real * twist_sin
    wave_cos, wave_sin = turn_table(line_index, line_index, length)
    spec_real = right_dot(turned_real, wave_cos) + right_dot(turned_imag, wave_sin)
    spec_imag = right_dot(turned_imag, wave_cos) - right_dot(turned_real, wave_sin)
    mixed_real, filter_real, carry_real = (spec_real[0], spec_real[1], spec_real[2])
    mixed_imag, filter_imag, carry_imag = (spec_imag[0], spec_imag[1], spec_imag[2])
    prod_real = jnp.stack(
        [
            filter_real * mixed_real - filter_imag * mixed_imag,
            filter_real * carry_real + filter_imag * carry_imag,
            mixed_real * carry_real + mixed_imag * carry_imag,
        ]
    )
    prod_imag = jnp.stack(
        [
            filter_real * mixed_imag + filter_imag * mixed_real,
            filter_real * carry_imag - filter_imag * carry_real,
            mixed_real * carry_imag - mixed_imag * carry_real,
        ]
    )
    back_real = right_dot(prod_real, wave_cos) - right_dot(prod_imag, wave_sin)
    back_imag = right_dot(prod_real, wave_sin) + right_dot(prod_imag, wave_cos)
    reverted_real = back_real * twist_cos - back_imag * twist_sin
    reverted_imag = back_real * twist_sin + back_imag * twist_cos
    packed = jnp.stack([reverted_real, reverted_imag])
    returned = lax.all_to_all(
        packed.reshape(2, 3, channels, 2, blocks, shards),
        "ctx",
        split_axis=5,
        concat_axis=5,
        tiled=True,
    )
    inv_real = jnp.stack([cosine, cosine * parity[None, :]])
    inv_imag = jnp.stack([-sines, -sines * parity[None, :]])
    timed = jnp.einsum("scjbk,jkm->scbm", returned[0], inv_real, precision=HIGHEST)
    timed = timed + jnp.einsum("scjbk,jkm->scbm", returned[1], inv_imag, precision=HIGHEST)
    timed = timed * (1.0 / period)
    result = lax.all_to_all(timed, "ctx", split_axis=3, concat_axis=3, tiled=True).reshape(
        3, channels, length
    )
    gain = skip_gain[:, None]
    before = result[0] + gain * mixed
    output = second * before
    grad_second = grad_output.astype(jnp.float32) * before
    back_mixed = result[1] + gain * carried
    grad_first = back_mixed * values_wide
    grad_values = back_mixed * first
    grad_filters = result[2]
    grad_skip = lax.psum(jnp.sum(carried * mixed, axis=1), "ctx")
    return (output, grad_first, grad_second, grad_values, grad_filters, grad_skip)


def per_device(first_gate, second_gate, values, filters, skip_gain, grad_output):
    channels, blocks = filters.shape
    shards = lax.axis_size("ctx")
    fits = channels == ROWS * shards and shards & (shards - 1) == 0 and blocks % LANES == 0 and channels <= LANES
    plan = by_channels if fits else by_columns
    return plan(first_gate, second_gate, values, filters, skip_gain, grad_output)


def solution(mesh):
    placed = (
        P("chan", ("groups", "ctx")),
        P("chan", ("groups", "ctx")),
        P("chan", ("groups", "ctx")),
        P("chan", ("groups", "ctx")),
        P("chan"),
        P("chan", ("groups", "ctx")),
    )
    return jax.shard_map(
        per_device,
        mesh=mesh,
        in_specs=placed,
        out_specs=(
            P("chan", ("groups", "ctx")),
            P("chan", ("groups", "ctx")),
            P("chan", ("groups", "ctx")),
            P("chan", ("groups", "ctx")),
            P("chan", ("groups", "ctx")),
            P(("groups", "chan")),
        ),
        check_vma=False,
    )
```

```python
import math

import jax
import jax.numpy as jnp
import numpy as np
from jax import lax
from jax.experimental import pallas as pl
from jax.experimental.pallas import tpu as pltpu
from jax.sharding import PartitionSpec as P

HIGHEST = lax.Precision.HIGHEST
OUTWARD = ((6, 7), (1, 3), (2,), (5,), (4,))
HOMEWARD = ((6, 7), (1, 3), (4,), (2,), (5,))
LANES = 128
ROWS = 8
VMEM = pl.BlockSpec(memory_space=pltpu.VMEM)
HBM = pl.BlockSpec(memory_space=pltpu.HBM)
PARAMS = pltpu.CompilerParams(vmem_limit_bytes=48 * 1024 * 1024)


def make_tables(length):
    groups = length // LANES
    period = 2 * length
    turns = 2 * groups
    k1 = np.arange(groups + 1)
    inner = k1[1:-1]
    a = np.arange(groups)
    b = np.arange(LANES)
    cosine = np.cos(2.0 * np.pi / turns * (k1[:, None] * a % turns))
    sine = np.sin(2.0 * np.pi / turns * (inner[:, None] * a % turns))
    weight = np.where((k1 == 0) | (k1 == groups), 1.0, 2.0) / period
    outer = np.concatenate([cosine, sine])
    back = np.concatenate([weight[:, None] * cosine, -2.0 / period * sine]).T
    wave = 2.0 * np.pi / LANES * (b[:, None] * b % LANES)
    twist = 2.0 * np.pi / period * (k1[:, None] * b % period)
    parts = [np.repeat(outer, ROWS, axis=1), np.repeat(back, ROWS, axis=1)]
    parts = [np.concatenate(np.split(part, part.shape[1] // LANES, axis=1)) for part in parts]
    parts += [np.cos(wave), np.sin(wave), np.cos(twist), np.sin(twist)]
    parts.append(np.zeros((-2 * (groups + 1) % ROWS, LANES)))
    return np.concatenate(parts).astype(np.float32)


def spread_rows(table, masked):
    rows, columns = table.shape
    wide = jnp.broadcast_to(table[:, None, :], (rows, ROWS, columns))
    if masked:
        shape = (ROWS, columns)
        own = lax.broadcasted_iota(jnp.int32, shape, 0) == lax.broadcasted_iota(jnp.int32, shape, 1) % ROWS
        wide = jnp.where(own[None], wide, 0.0)
    return wide.reshape(rows * ROWS, columns)


def split(data):
    high = data.astype(jnp.bfloat16)
    return high, (data - high.astype(jnp.float32)).astype(jnp.bfloat16)


def dot(left, right):
    return jnp.dot(left, right, preferred_element_type=jnp.float32)


def long_dot(left, right):
    return dot(left[0], right[0]) + (dot(left[0], right[1]) + dot(left[1], right[0]))


def table_dot(table, data):
    high, low = split(data)
    both = dot(table[0], jnp.concatenate([high, low], axis=1))
    columns = data.shape[1]
    return both[:, :columns] + (both[:, columns:] + dot(table[1], high))


def table_kernel(in_ref, outer_ref, back_ref, forward_ref, inverse_ref, twist_ref):
    groups = outer_ref.shape[2] // ROWS
    tiles = outer_ref.shape[2] // LANES
    row = 0

    def take(rows, pieces=1):
        nonlocal row
        parts = [in_ref[row + i * rows : row + (i + 1) * rows, :] for i in range(pieces)]
        row += rows * pieces
        return jnp.concatenate(parts, axis=1)

    outer_ref[0], outer_ref[1] = split(spread_rows(take(2 * groups, tiles), True))
    back_ref[0], back_ref[1] = split(spread_rows(take(groups, 2 * tiles), True))
    cosine, sine = split(take(LANES)), split(take(LANES))
    for i, (c, s) in enumerate(zip(cosine, sine)):
        forward_ref[i] = jnp.concatenate([jnp.concatenate([c, -s], axis=1), jnp.concatenate([s, c], axis=1)], axis=0)
        inverse_ref[i] = jnp.concatenate([jnp.concatenate([c, s], axis=1), jnp.concatenate([-s, c], axis=1)], axis=0)
    twist_ref[0] = spread_rows(take(groups + 1), False)
    twist_ref[1] = spread_rows(take(groups + 1), False)


def sent(shards, groups):
    if sum(map(len, groups)) != shards - 1:
        groups = tuple((turn,) for turn in range(shards - 1, 0, -1))
    return (*groups, (0,))


def received(shards, groups):
    groups = sent(shards, groups)
    first = [(group[0], *(None for _ in group[1:])) for group in groups]
    return (*first[:-1], *((turn,) for group in groups for turn in group[1:]), (0,))


def swap(arrays, groups):
    *arrays, own = arrays
    shards = lax.axis_size("ctx")

    def move(array, turn):
        return lax.ppermute(array, "ctx", [(i, i ^ turn) for i in range(shards)])

    moved, relayed = [], []
    for members, array in zip(sent(shards, groups), arrays):
        moved.append(move(array, members[0]))
        relayed += [move(moved[-1][i : i + 1], members[0] ^ members[i]) for i in range(1, len(members))]
    return (*moved, *relayed, own)


def gather(place_ref, in_refs, groups):
    me = lax.axis_index("ctx")
    for members, ref in zip(received(place_ref.shape[0], groups), in_refs):
        for i, turn in enumerate(members):
            if turn is not None:
                place_ref[me ^ turn] = ref[i]


def scatter(out_refs, place_ref, groups):
    me = lax.axis_index("ctx")
    for members, ref in zip(sent(place_ref.shape[0], groups), out_refs):
        for i, turn in enumerate(members):
            ref[i] = place_ref[me ^ turn]


def gate_kernel(first_hbm, values_hbm, grad_hbm, second_hbm, filters_hbm, gain_hbm, *refs):
    *out_refs, kept_ref, all_ref, filters_ref, gain_ref, sems = refs
    gates = [kept_ref.at[i] for i in range(4)]
    sources = (first_hbm, values_hbm, filters_hbm, gain_hbm, grad_hbm, second_hbm)
    places = (*gates[:2], filters_ref, gain_ref, *gates[2:])
    copies = [pltpu.make_async_copy(source, place, sems.at[i]) for i, (source, place) in enumerate(zip(sources, places))]
    for copy in copies:
        copy.start()
    shards = all_ref.shape[0]
    channels, blocks = filters_ref.shape
    me = lax.axis_index("ctx")

    def place(s, signal):
        for j in range(blocks // LANES):
            tile = signal[:, j * LANES : (j + 1) * LANES].reshape(shards, ROWS, LANES)
            all_ref[:, s, :, j * LANES : (j + 1) * LANES] = tile
        for members, ref in zip(sent(shards, OUTWARD), out_refs):
            for i, turn in enumerate(members):
                ref[i, s] = all_ref[me ^ turn, s]

    copies[0].wait()
    copies[1].wait()
    place(0, kept_ref[0].astype(jnp.float32) * kept_ref[1].astype(jnp.float32))
    copies[2].wait()
    copies[3].wait()
    shape = (channels, channels)
    diagonal = lax.broadcasted_iota(jnp.int32, shape, 0) == lax.broadcasted_iota(jnp.int32, shape, 1)
    gain = jnp.sum(jnp.where(diagonal, gain_ref[...], 0.0), axis=1, keepdims=True)
    position = me * blocks + lax.broadcasted_iota(jnp.int32, (channels, blocks), 1)
    place(1, filters_ref[...] + jnp.where(position == 0, gain, 0.0))
    copies[4].wait()
    copies[5].wait()
    place(2, kept_ref[2].astype(jnp.float32) * kept_ref[3].astype(jnp.float32))


def spectral_kernel(outer_ref, back_ref, forward_ref, inverse_ref, twist_ref, *refs):
    *refs, all_ref, in_ref = refs
    shards = in_ref.shape[0]
    count = len(received(shards, OUTWARD))
    in_refs, out_refs = refs[:count], refs[count:]
    gather(in_ref, in_refs, OUTWARD)
    tiles = in_ref.shape[3] // LANES
    span = tiles * ROWS
    rows = shards * span
    spec_rows = rows + ROWS
    cosine, sine = twist_ref[0], twist_ref[1]

    def take(s):
        parts = [in_ref[:, s, :, j * LANES : (j + 1) * LANES] for j in range(tiles)]
        return jnp.stack(parts, axis=1).reshape(rows, LANES)

    signals = [take(s) for s in range(3)]
    total = jnp.sum((signals[0] * signals[2]).reshape(rows // ROWS, ROWS, LANES), axis=0)
    total = jnp.broadcast_to(jnp.sum(total, axis=1, keepdims=True), (ROWS, LANES))
    all_ref[:, 3 * span :, :] = jnp.broadcast_to(total[None], (shards, ROWS, LANES))
    columns = table_dot(outer_ref, jnp.concatenate(signals, axis=1))
    edge = jnp.zeros((ROWS, LANES), jnp.float32)
    spectra = []
    for s in range(3):
        lanes = slice(s * LANES, (s + 1) * LANES)
        real = columns[:spec_rows, lanes]
        imag = jnp.concatenate([edge, columns[spec_rows:, lanes], edge], axis=0)
        turned = jnp.concatenate([real * cosine - imag * sine, -(real * sine + imag * cosine)], axis=1)
        spectra.append(long_dot(split(turned), forward_ref))
    (mr, mi), (fr, fi), (cr, ci) = [(x[:, :LANES], x[:, LANES:]) for x in spectra]
    products = (
        (fr * mr - fi * mi, fr * mi + fi * mr),
        (fr * cr + fi * ci, fr * ci - fi * cr),
        (mr * cr + mi * ci, mr * ci - mi * cr),
    )
    reverted = []
    for real, imag in products:
        waves = long_dot(split(jnp.concatenate([real, imag], axis=1)), inverse_ref)
        real, imag = waves[:, :LANES], waves[:, LANES:]
        turned_imag = real * sine + imag * cosine
        reverted.append(jnp.concatenate([real * cosine - imag * sine, turned_imag[ROWS:-ROWS]], axis=0))
    result = table_dot(back_ref, jnp.concatenate(reverted, axis=1))
    for s in range(3):
        all_ref[:, s * span : (s + 1) * span, :] = result[:, s * LANES : (s + 1) * LANES].reshape(shards, span, LANES)
    scatter(out_refs, all_ref, HOMEWARD)


def output_kernel(kept_ref, *refs):
    _, channels, blocks = kept_ref.shape
    tiles = blocks // LANES
    count = len(received(channels // ROWS, HOMEWARD))
    in_refs, (out_ref, gfirst_ref, gsecond_ref, gvalues_ref, gfilters_ref, gskip_ref, result_ref, total_ref) = refs[:count], refs[count:]
    me = lax.axis_index("ctx")
    for members, ref in zip(received(channels // ROWS, HOMEWARD), in_refs):
        for i, turn in enumerate(members):
            if turn is None:
                continue
            own = pl.ds(pl.multiple_of((me ^ turn) * ROWS, ROWS), ROWS)
            for s, dst_ref in enumerate((result_ref.at[0], result_ref.at[1], gfilters_ref)):
                for j in range(tiles):
                    dst_ref[own, j * LANES : (j + 1) * LANES] = ref[i, (s * tiles + j) * ROWS : (s * tiles + j + 1) * ROWS, :]
            total_ref[own, :] = ref[i, 3 * tiles * ROWS :, :]
    first, values, grad, second = [kept_ref[i].astype(jnp.float32) for i in range(4)]
    before = result_ref[0]
    out_ref[...] = second * before
    gsecond_ref[...] = grad * before
    back = result_ref[1]
    gfirst_ref[...] = back * values
    gvalues_ref[...] = back * first
    shape = (channels, channels)
    diagonal = lax.broadcasted_iota(jnp.int32, shape, 0) == lax.broadcasted_iota(jnp.int32, shape, 1)
    gskip_ref[...] = jnp.sum(jnp.where(diagonal, total_ref[:, :channels], 0.0), axis=0, keepdims=True)


def call(kernel, out_shape, args, scratch_shapes=()):
    return pl.pallas_call(
        kernel,
        out_shape=out_shape,
        in_specs=[VMEM] * len(args),
        out_specs=[VMEM] * len(out_shape),
        scratch_shapes=scratch_shapes,
        compiler_params=PARAMS,
    )(*args)


def by_channels(first_gate, second_gate, values, filters, skip_gain, grad_output):
    channels, blocks = filters.shape
    shards = lax.axis_size("ctx")
    tiles = blocks // LANES
    length = blocks * shards
    rows = length // LANES * ROWS
    wide, half = jnp.float32, jnp.bfloat16
    sources = (first_gate, values, grad_output, second_gate, filters, skip_gain.reshape(1, channels))
    slab = (3, ROWS, blocks)
    outs = [pltpu.VMEM((len(members), *slab), wide) for members in sent(shards, OUTWARD)]
    *slabs, kept = pl.pallas_call(
        gate_kernel,
        out_shape=[*outs, pltpu.VMEM((4, channels, blocks), half)],
        in_specs=[HBM] * len(sources),
        out_specs=[VMEM] * (len(outs) + 1),
        scratch_shapes=[
            pltpu.VMEM((shards, *slab), wide),
            pltpu.VMEM((channels, blocks), wide),
            pltpu.VMEM((1, channels), wide),
            pltpu.SemaphoreType.DMA((len(sources),)),
        ],
        compiler_params=PARAMS,
    )(*[pltpu.with_memory_space_constraint(source, pltpu.HBM) for source in sources])
    tables = call(
        table_kernel,
        [
            pltpu.VMEM((2, 2 * rows, rows), half),
            pltpu.VMEM((2, rows, 2 * rows), half),
            pltpu.VMEM((2, 2 * LANES, 2 * LANES), half),
            pltpu.VMEM((2, 2 * LANES, 2 * LANES), half),
            pltpu.VMEM((2, rows + ROWS, LANES), wide),
        ],
        [jnp.asarray(make_tables(length))],
    )
    result = ((3 * tiles + 1) * ROWS, LANES)
    slabs = call(
        spectral_kernel,
        [pltpu.VMEM((len(members), *result), wide) for members in sent(shards, HOMEWARD)],
        (*tables, *swap(slabs, OUTWARD)),
        [pltpu.VMEM((shards, *result), wide), pltpu.VMEM((shards, *slab), wide)],
    )
    *full, grad_skip = call(
        output_kernel,
        [jax.ShapeDtypeStruct((channels, blocks), wide)] * 5 + [jax.ShapeDtypeStruct((1, channels), wide)],
        (kept, *swap(slabs, HOMEWARD)),
        [pltpu.VMEM((2, channels, blocks), wide), pltpu.VMEM((channels, LANES), wide)],
    )
    return (*full, grad_skip.reshape(channels))


def turn_table(first_index, second_index, period):
    product = first_index[:, None] * second_index[None, :] % period
    angles = 2.0 * math.pi / period * product.astype(jnp.float32)
    return (jnp.cos(angles), jnp.sin(angles))


def right_dot(data, table):
    return jnp.dot(data, table, precision=HIGHEST)


def by_columns(first_gate, second_gate, values, filters, skip_gain, grad_output):
    channels, length = filters.shape
    shards = lax.axis_size("ctx")
    blocks = length // shards
    position = lax.axis_index("ctx")
    period = 2 * shards * length
    first = first_gate.astype(jnp.float32)
    second = second_gate.astype(jnp.float32)
    values_wide = values.astype(jnp.float32)
    mixed = first * values_wide
    carried = grad_output.astype(jnp.float32) * second
    signal = jnp.stack([mixed, filters, carried]).reshape(3, channels, blocks, shards)
    spread = lax.all_to_all(signal, "ctx", split_axis=3, concat_axis=3, tiled=True)
    shard_index = jnp.arange(shards, dtype=jnp.int32)
    cosine, sines = turn_table(shard_index, shard_index, 2 * shards)
    parity = (1 - 2 * (shard_index % 2)).astype(jnp.float32)
    fwd_real = jnp.stack([cosine, parity[:, None] * cosine], axis=1)
    fwd_imag = jnp.stack([-sines, -parity[:, None] * sines], axis=1)
    real_part = jnp.einsum("scbm,mjk->scjbk", spread, fwd_real, precision=HIGHEST)
    imag_part = jnp.einsum("scbm,mjk->scjbk", spread, fwd_imag, precision=HIGHEST)
    sectioned = jnp.stack([real_part, imag_part])
    moved = lax.all_to_all(sectioned, "ctx", split_axis=5, concat_axis=5, tiled=True).reshape(
        2, 3, channels, 2, length
    )
    col_real = moved[0]
    col_imag = moved[1]
    col_index = jnp.stack([position, position + shards])
    line_index = jnp.arange(length, dtype=jnp.int32)
    twist_cos, twist_sin = turn_table(col_index, line_index, period)
    turned_real = col_real * twist_cos + col_imag * twist_sin
    turned_imag = col_imag * twist_cos - col_real * twist_sin
    wave_cos, wave_sin = turn_table(line_index, line_index, length)
    spec_real = right_dot(turned_real, wave_cos) + right_dot(turned_imag, wave_sin)
    spec_imag = right_dot(turned_imag, wave_cos) - right_dot(turned_real, wave_sin)
    mixed_real, filter_real, carry_real = (spec_real[0], spec_real[1], spec_real[2])
    mixed_imag, filter_imag, carry_imag = (spec_imag[0], spec_imag[1], spec_imag[2])
    prod_real = jnp.stack(
        [
            filter_real * mixed_real - filter_imag * mixed_imag,
            filter_real * carry_real + filter_imag * carry_imag,
            mixed_real * carry_real + mixed_imag * carry_imag,
        ]
    )
    prod_imag = jnp.stack(
        [
            filter_real * mixed_imag + filter_imag * mixed_real,
            filter_real * carry_imag - filter_imag * carry_real,
            mixed_real * carry_imag - mixed_imag * carry_real,
        ]
    )
    back_real = right_dot(prod_real, wave_cos) - right_dot(prod_imag, wave_sin)
    back_imag = right_dot(prod_real, wave_sin) + right_dot(prod_imag, wave_cos)
    reverted_real = back_real * twist_cos - back_imag * twist_sin
    reverted_imag = back_real * twist_sin + back_imag * twist_cos
    packed = jnp.stack([reverted_real, reverted_imag])
    returned = lax.all_to_all(
        packed.reshape(2, 3, channels, 2, blocks, shards),
        "ctx",
        split_axis=5,
        concat_axis=5,
        tiled=True,
    )
    inv_real = jnp.stack([cosine, cosine * parity[None, :]])
    inv_imag = jnp.stack([-sines, -sines * parity[None, :]])
    timed = jnp.einsum("scjbk,jkm->scbm", returned[0], inv_real, precision=HIGHEST)
    timed = timed + jnp.einsum("scjbk,jkm->scbm", returned[1], inv_imag, precision=HIGHEST)
    timed = timed * (1.0 / period)
    result = lax.all_to_all(timed, "ctx", split_axis=3, concat_axis=3, tiled=True).reshape(
        3, channels, length
    )
    gain = skip_gain[:, None]
    before = result[0] + gain * mixed
    output = second * before
    grad_second = grad_output.astype(jnp.float32) * before
    back_mixed = result[1] + gain * carried
    grad_first = back_mixed * values_wide
    grad_values = back_mixed * first
    grad_filters = result[2]
    grad_skip = lax.psum(jnp.sum(carried * mixed, axis=1), "ctx")
    return (output, grad_first, grad_second, grad_values, grad_filters, grad_skip)


def per_device(first_gate, second_gate, values, filters, skip_gain, grad_output):
    channels, blocks = filters.shape
    shards = lax.axis_size("ctx")
    fits = channels == ROWS * shards and shards & (shards - 1) == 0 and blocks % LANES == 0 and channels <= LANES
    plan = by_channels if fits else by_columns
    return plan(first_gate, second_gate, values, filters, skip_gain, grad_output)


def solution(mesh):
    placed = (
        P("chan", ("groups", "ctx")),
        P("chan", ("groups", "ctx")),
        P("chan", ("groups", "ctx")),
        P("chan", ("groups", "ctx")),
        P("chan"),
        P("chan", ("groups", "ctx")),
    )
    return jax.shard_map(
        per_device,
        mesh=mesh,
        in_specs=placed,
        out_specs=(
            P("chan", ("groups", "ctx")),
            P("chan", ("groups", "ctx")),
            P("chan", ("groups", "ctx")),
            P("chan", ("groups", "ctx")),
            P("chan", ("groups", "ctx")),
            P(("groups", "chan")),
        ),
        check_vma=False,
    )
```
